128 devices in a mesh: grp: 4 (over y_hi, core), dev: 32 (over x, z, y_lo).
Axes of the slice: x: 4, y: 4 (y_hi: 2, y_lo: 2; y = y_hi * 2 + y_lo), z: 4, core: 2. Of those that a mesh axis runs over, the one named last changes fastest.
Arguments:
- x_feat: float32 [64, 32768], P(None, 'dev'), may hold values from -4 to 4
- y_feat: float32 [64, 65536], P(None, ('grp', 'dev')), may hold values from -4 to 4
Outputs:
- dual_row: float32 [32768], P('dev')
- dual_col: float32 [65536], P('grp')
The draws below stay inside these ranges and needn't reach their ends.
All inputs are finite; a program needn't handle non-finite values.
Results may differ from the reference program's by a relative error of at most 0.0003.
Values sent between devices are 32-bit elements; how exact they have to be, the bound alone decides.
No kernel may reach another device: no remote copies, remote signals or barrier semaphores. Data moves between devices by JAX's collectives and lax.ppermute only.
A program may use at most 64 MiB of HBM per device.

```python
import math
import jax
import jax.numpy as jnp
from jax import lax

DIM = 64
ITERS = 2
N = 32768
M = 65536


def draw_x_feat(key, part):
    key = jax.random.fold_in(key, 11)
    values = jax.random.normal(key, (DIM, N), jnp.float32) * 0.2
    return jnp.clip(values, -4.0, 4.0)


def draw_y_feat(key, part):
    key = jax.random.fold_in(key, 23)
    values = jax.random.normal(key, (DIM, M), jnp.float32) * 0.2
    return jnp.clip(values, -4.0, 4.0)


def setup_inputs(seed: int = 0) -> dict:
    splits = jax.random.split(jax.random.key(seed), 3)
    return {
        "x_feat": draw_x_feat(jax.random.fold_in(splits[2], 71), 0),
        "y_feat": draw_y_feat(jax.random.fold_in(splits[2], 71), 0),
    }


eps_value = 0.5
block_width = 1024


def pair_cost(source, source_sq, target):
    target_sq = jnp.sum(target * target, axis=0)
    cross = lax.dot_general(source, target, (((0,), (0,)), ((), ())), precision=lax.Precision.HIGHEST, preferred_element_type=jnp.float32)
    return source_sq[:, None] + target_sq[None, :] - 2.0 * cross


def split_blocks(target, dual):
    width = target.shape[1]
    step = min(block_width, width)
    count = width // step
    return target.reshape(target.shape[0], count, step).transpose(1, 0, 2), dual.reshape(count, step)


def row_lse(source, target, dual):
    source_sq = jnp.sum(source * source, axis=0)
    blocks, duals = split_blocks(target, dual)
    rows = source.shape[1]

    def advance(carry, item):
        peak, total = carry
        tblock, dblock = item
        score = (dblock[None, :] - pair_cost(source, source_sq, tblock)) / eps_value
        new_peak = jnp.maximum(peak, jnp.max(score, axis=1))
        total = total * jnp.exp(peak - new_peak) + jnp.sum(jnp.exp(score - new_peak[:, None]), axis=1)
        return (new_peak, total), None

    init = (jnp.full((rows,), -1e30, jnp.float32), jnp.zeros((rows,), jnp.float32))
    result, unused = lax.scan(advance, init, (blocks, duals))
    return result


def col_lse(source, target, dual):
    source_sq = jnp.sum(source * source, axis=0)
    blocks, unused = split_blocks(target, jnp.zeros((target.shape[1],), jnp.float32))

    def column_block(tblock):
        score = (dual[:, None] - pair_cost(source, source_sq, tblock)) / eps_value
        peak = jnp.max(score, axis=0)
        total = jnp.sum(jnp.exp(score - peak[None, :]), axis=0)
        return peak, total

    peak, total = lax.map(column_block, blocks)
    return peak.reshape(-1), total.reshape(-1)


def reference(x_feat, y_feat):
    count_src = x_feat.shape[1]
    count_tgt = y_feat.shape[1]
    dual_col = jnp.zeros((count_tgt,), jnp.float32)
    dual_row = jnp.zeros((count_src,), jnp.float32)
    for iteration in range(ITERS):
        peak, total = row_lse(x_feat, y_feat, dual_col)
        dual_row = -eps_value * (peak + jnp.log(total)) + eps_value * math.log(count_tgt)
        peak, total = col_lse(x_feat, y_feat, dual_row)
        dual_col = -eps_value * (peak + jnp.log(total)) + eps_value * math.log(count_src)
    return dual_row, dual_col
```

```python
import math

import jax
import jax.numpy as jnp
from jax import lax
from jax.experimental import pallas as pl
from jax.experimental.pallas import tpu as pltpu
from jax.sharding import Mesh
from jax.sharding import PartitionSpec as P

ITERS = 2
EPS = 0.5
LOG2E = 1.0 / math.log(2.0)
SCALE = LOG2E / EPS

LANES = 128
CHUNK = 256
WIDTH = 256
ACC_ROWS = 16
DUAL_LANE = 64

f32 = jnp.float32
bf16 = jnp.bfloat16
vmem = pl.BlockSpec(memory_space=pltpu.VMEM)


def split2(value):
    high = value.astype(bf16)
    return high, (value - high.astype(f32)).astype(bf16)


def fold(op, acc, value):
    rows = acc.shape[0]
    for i in range(value.shape[0] // rows):
        acc = op(acc, value[i * rows : (i + 1) * rows])
    return acc


def prepare_side(src, main, tail, rhs, norm, scale):
    blocks, dim, cells = src.shape
    for b in range(blocks):
        value = src[b]
        square = jnp.sum(value * value, axis=0, keepdims=True)
        for q in range(cells // LANES):
            row = b * (cells // LANES) + q
            norm[row : row + 1, :] = square[:, q * LANES : (q + 1) * LANES]
        high, low = split2(value * scale)
        here = pl.ds(b * cells, cells)
        rhs[0:dim, here] = high
        rhs[dim : 2 * dim, here] = low
        rhs[2 * dim : 3 * dim, here] = high
        place = lax.broadcasted_iota(jnp.int32, (dim, cells), 0)
        rhs[3 * dim : 4 * dim, here] = jnp.where(place < 3, 1.0, 0.0).astype(bf16)
        main[here, :] = jnp.transpose(jnp.concatenate([high, high], axis=0))
        tail[here, :] = jnp.transpose(jnp.concatenate([low, jnp.zeros_like(low)], axis=0))


def prepare_kernel(log_src, x_ref, y_ref, xm, xt, xr, xn, ym, yt, yr, yn, first):
    prepare_side(x_ref, xm, xt, xr, xn, 2.0 * SCALE)
    prepare_side(y_ref, ym, yt, yr, yn, 1.0)
    first[0] = log_src + SCALE * yn[...]


def combine(parts, log_count):
    peak = parts[0]
    for i in range(1, parts.shape[0]):
        peak = jnp.maximum(peak, parts[i])
    total = jnp.exp2(parts[0] - peak)
    for i in range(1, parts.shape[0]):
        total = total + jnp.exp2(parts[i] - peak)
    return log_count - (peak + jnp.log2(total))


def pass_kernel(log_count, parts, main, tail, rhs, out, *rest):
    full, score = rest[-2:]
    length, width = main.shape[0], rhs.shape[1]
    dual = combine(parts, log_count)
    if len(rest) == 4:
        norm, dual_out = rest[:2]
        dual_out[...] = dual * (1.0 / SCALE) + norm[...]
    high = dual.astype(bf16).astype(f32)
    mid = (dual - high).astype(bf16).astype(f32)
    low = dual - high - mid
    place = lax.broadcasted_iota(jnp.int32, (LANES, LANES), 0)
    for k in range(length // LANES):
        here = pl.ds(k * LANES, LANES)
        rows = jnp.where(place == DUAL_LANE, high[k : k + 1], 0.0)
        rows = jnp.where(place == DUAL_LANE + 1, mid[k : k + 1], rows)
        rows = jnp.where(place == DUAL_LANE + 2, low[k : k + 1], rows)
        full[here, :] = (tail[here, :].astype(f32) + jnp.transpose(rows)).astype(bf16)

    def scores(block, chunk, peak):
        here = pl.ds(chunk * CHUNK, CHUNK)
        lhs = jnp.concatenate([main[here, :], full[here, :]], axis=1)
        cols = pl.ds(pl.multiple_of(block * WIDTH, WIDTH), WIDTH)
        value = jnp.dot(lhs, rhs[:, cols], preferred_element_type=f32)
        score[here, :] = value
        return fold(jnp.maximum, peak, value)

    def sums(chunk, top, acc):
        here = pl.ds(chunk * CHUNK, CHUNK)
        return fold(jnp.add, acc, jnp.exp2(score[here, :] - top))

    def finish(block, top, acc):
        value = top + jnp.log2(jnp.sum(acc, axis=0, keepdims=True))
        for q in range(WIDTH // LANES):
            row = block * (WIDTH // LANES) + q
            piece = value[:, q * LANES : (q + 1) * LANES][None]
            out[:, pl.ds(row, 1), :] = jnp.broadcast_to(piece, (out.shape[0], 1, LANES))

    chunks, blocks = length // CHUNK, width // WIDTH
    lowest = jnp.full((ACC_ROWS, WIDTH), -jnp.inf, f32)
    zero = jnp.zeros((ACC_ROWS, WIDTH), f32)

    peak = lowest
    for chunk in range(chunks):
        peak = scores(0, chunk, peak)

    def step(block, top):
        peak, acc = lowest, zero
        for chunk in range(chunks):
            acc = sums(chunk, top, acc)
            peak = scores(block, chunk, peak)
        finish(block - 1, top, acc)
        return jnp.max(peak, axis=0, keepdims=True)

    top = lax.fori_loop(1, blocks, step, jnp.max(peak, axis=0, keepdims=True))
    acc = zero
    for chunk in range(chunks):
        acc = sums(chunk, top, acc)
    finish(blocks - 1, top, acc)


def final_kernel(log_count, parts, norm, out):
    value = combine(parts, log_count) * (1.0 / SCALE) + norm[...]
    for i in range(out.shape[0]):
        out[i] = value


def params(mib):
    return pltpu.CompilerParams(vmem_limit_bytes=mib * 2**20)


def lse_pass(log_count, parts, main, tail, rhs, copies, norm=None):
    length, width = main.shape[0], rhs.shape[1]
    out = jax.ShapeDtypeStruct((copies, width // LANES, LANES), f32)
    scratch = [pltpu.VMEM((length, LANES), bf16), pltpu.VMEM((length, WIDTH), f32)]
    if norm is None:
        return pl.pallas_call(
            lambda *refs: pass_kernel(log_count, *refs),
            out_shape=out,
            in_specs=[vmem] * 4,
            out_specs=vmem,
            scratch_shapes=scratch,
            compiler_params=params(20),
        )(parts, main, tail, rhs)

    def kernel(parts, main, tail, rhs, norm, out, dual_out, full, score):
        pass_kernel(log_count, parts, main, tail, rhs, out, norm, dual_out, full, score)

    return pl.pallas_call(
        kernel,
        out_shape=(out, jax.ShapeDtypeStruct((length // LANES, LANES), f32)),
        in_specs=[vmem] * 5,
        out_specs=(vmem, vmem),
        scratch_shapes=scratch,
        compiler_params=params(20),
    )(parts, main, tail, rhs, norm)


def gathered(value, axes):
    copies = jnp.broadcast_to(value[None], (lax.axis_size(axes),) + value.shape)
    return lax.all_to_all(copies, axes, 0, 0, tiled=True)


def exchanged(parts, axes):
    return lax.all_to_all(parts, axes, 0, 0, tiled=True)


ROW_GATHER = "x"
COL_GATHER = ("z", "yl")
ROW_PEERS = ("yh", "core", "x")
COL_PEERS = ("z", "yl")


def on_device(x_feat, y_feat):
    xg = gathered(x_feat, ROW_GATHER)
    yg = gathered(y_feat, COL_GATHER)
    rows, cols = xg.shape[0] * xg.shape[2], yg.shape[0] * yg.shape[2]
    row_peers, col_peers = lax.axis_size(ROW_PEERS), lax.axis_size(COL_PEERS)
    log_tgt = math.log2(cols * row_peers)
    log_src = math.log2(rows * col_peers)

    def side(cells):
        return [
            jax.ShapeDtypeStruct((cells, LANES), bf16),
            jax.ShapeDtypeStruct((cells, LANES), bf16),
            jax.ShapeDtypeStruct((4 * x_feat.shape[0], cells), bf16),
            jax.ShapeDtypeStruct((cells // LANES, LANES), f32),
        ]

    xm, xt, xr, xn, ym, yt, yr, yn, parts = pl.pallas_call(
        lambda *refs: prepare_kernel(log_src, *refs),
        out_shape=side(rows) + side(cols) + [jax.ShapeDtypeStruct((1, cols // LANES, LANES), f32)],
        in_specs=[vmem] * 2,
        out_specs=[vmem] * 9,
        compiler_params=params(20),
    )(xg, yg)
    for iteration in range(ITERS):
        parts = exchanged(lse_pass(log_src, parts, ym, yt, xr, row_peers), ROW_PEERS)
        sums, dual_row = lse_pass(log_tgt, parts, xm, xt, yr, col_peers, xn)
        parts = exchanged(sums, COL_PEERS)
    own = x_feat.shape[1] // LANES
    dual_row = lax.dynamic_slice_in_dim(dual_row, lax.axis_index(ROW_GATHER) * own, own, 0)
    spread = lax.axis_size(ROW_GATHER)
    dual_col = pl.pallas_call(
        lambda *refs: final_kernel(log_src, *refs),
        out_shape=jax.ShapeDtypeStruct((spread, cols // LANES, LANES), f32),
        in_specs=[vmem] * 2,
        out_specs=vmem,
    )(parts, yn)
    dual_col = exchanged(dual_col, ROW_GATHER)
    return dual_row.reshape(-1), dual_col.reshape(-1)


def solution(mesh):
    fine = Mesh(mesh.devices.reshape(2, 2, 4, 4, 2), ("yh", "core", "x", "z", "yl"))
    dev = ("x", "z", "yl")
    in_specs = (P(None, dev), P(None, ("yh", "core") + dev))
    out_specs = (P(dev), P(("yh", "core")))
    return jax.shard_map(
        on_device, mesh=fine, in_specs=in_specs, out_specs=out_specs, check_vma=False
    )
```

```python
import math

import jax
import jax.numpy as jnp
from jax import lax
from jax.experimental import pallas as pl
from jax.experimental.pallas import tpu as pltpu
from jax.sharding import Mesh
from jax.sharding import PartitionSpec as P

ITERS = 2
EPS = 0.5
LOG2E = 1.0 / math.log(2.0)
SCALE = LOG2E / EPS

LANES = 128
CHUNK = 256
WIDTH = 256
GROUP = 4
ACC_ROWS = 16
DUAL_LANE = 64
EDGE = 64
SMALLEST = 2.0**-80

f32 = jnp.float32
bf16 = jnp.bfloat16
vmem = pl.BlockSpec(memory_space=pltpu.VMEM)


def split2(value):
    high = value.astype(bf16)
    return high, (value - high.astype(f32)).astype(bf16)


def fold(op, acc, value):
    rows = acc.shape[0]
    for i in range(value.shape[0] // rows):
        acc = op(acc, value[i * rows : (i + 1) * rows])
    return acc


def prepare_side(src, main, tail, rhs, norm, scale):
    blocks, dim, cells = src.shape
    for b in range(blocks):
        value = src[b]
        square = jnp.sum(value * value, axis=0, keepdims=True)
        for q in range(cells // LANES):
            row = b * (cells // LANES) + q
            norm[row : row + 1, :] = square[:, q * LANES : (q + 1) * LANES]
        high, low = split2(value * scale)
        here = pl.ds(b * cells, cells)
        rhs[0:dim, here] = high
        rhs[dim : 2 * dim, here] = low
        rhs[2 * dim : 3 * dim, here] = high
        main[here, :] = jnp.transpose(jnp.concatenate([high, high], axis=0))
        tail[here, :] = jnp.transpose(jnp.concatenate([low, jnp.zeros_like(low)], axis=0))


def prepare_kernel(log_src, x_ref, y_ref, xm, xt, xr, xn, ym, yt, yr, yn, first, before):
    prepare_side(x_ref, xm, xt, xr, xn, 2.0 * SCALE)
    prepare_side(y_ref, ym, yt, yr, yn, 1.0)
    first[0] = log_src + SCALE * yn[...]
    before[...] = log_src - SCALE * xn[...]


def combine(parts, log_count):
    peak = parts[0]
    for i in range(1, parts.shape[0]):
        peak = jnp.maximum(peak, parts[i])
    total = jnp.exp2(parts[0] - peak)
    for i in range(1, parts.shape[0]):
        total = total + jnp.exp2(parts[i] - peak)
    return log_count - (peak + jnp.log2(total))


def split3(value):
    high = value.astype(bf16).astype(f32)
    mid = (value - high).astype(bf16).astype(f32)
    return high, mid, value - high - mid


def placed(parts, row, height, first):
    place = lax.broadcasted_iota(jnp.int32, (height, LANES), 0)
    value = jnp.zeros((height, LANES), f32)
    for i, part in enumerate(parts):
        value = jnp.where(place == first + i, part[row : row + 1], value)
    return value


def pass_kernel(log_count, parts, prev, main, tail, rhs, out, dual_out, full, edge, score):
    length, width = main.shape[0], rhs.shape[1]
    dual = combine(parts, log_count)
    dual_out[...] = dual
    bound = log_count - prev[...]
    duals, bounds = split3(dual), split3(-bound)
    place = lax.broadcasted_iota(jnp.int32, (LANES, LANES), 0)
    for k in range(length // LANES):
        here = pl.ds(k * LANES, LANES)
        rows = placed(duals, k, LANES, DUAL_LANE)
        rows = jnp.where((place >= DUAL_LANE + 3) & (place < DUAL_LANE + 6), 1.0, rows)
        full[here, :] = (tail[here, :].astype(f32) + jnp.transpose(rows)).astype(bf16)
    place = lax.broadcasted_iota(jnp.int32, (EDGE, LANES), 0)
    for k in range(width // LANES):
        rows = jnp.where(place < 3, 1.0, placed(bounds, k, EDGE, 3))
        edge[:, pl.ds(k * LANES, LANES)] = rows.astype(bf16)

    def scores(block, chunk):
        here = pl.ds(chunk * CHUNK, CHUNK)
        lhs = jnp.concatenate([main[here, :], full[here, :]], axis=1)
        cols = pl.ds(pl.multiple_of(block * WIDTH, WIDTH), WIDTH)
        weight = jnp.concatenate([rhs[:, cols], edge[:, cols]], axis=0)
        return jnp.dot(lhs, weight, preferred_element_type=f32)

    def finish(block, value):
        for q in range(WIDTH // LANES):
            row = block * (WIDTH // LANES) + q
            piece = value[:, q * LANES : (q + 1) * LANES][None]
            out[:, pl.ds(row, 1), :] = jnp.broadcast_to(piece, (out.shape[0], 1, LANES))

    chunks, blocks = length // CHUNK, width // WIDTH
    zero = jnp.zeros((ACC_ROWS, WIDTH), f32)

    def step(group, least):
        for t in range(GROUP):
            block = group * GROUP + t
            acc = zero
            for chunk in range(chunks):
                acc = fold(jnp.add, acc, jnp.exp2(scores(block, chunk)))
            total = jnp.sum(acc, axis=0, keepdims=True)
            least = jnp.minimum(least, total)
            finish(block, jnp.log2(total))
        return least

    least = lax.fori_loop(0, blocks // GROUP, step, jnp.full((1, WIDTH), 1.0, f32))

    @pl.when(jnp.min(least) < SMALLEST)
    def _():
        def exact(block, carry):
            peak = jnp.full((ACC_ROWS, WIDTH), -jnp.inf, f32)
            for chunk in range(chunks):
                value = scores(block, chunk)
                score[pl.ds(chunk * CHUNK, CHUNK), :] = value
                peak = fold(jnp.maximum, peak, value)
            top = jnp.max(peak, axis=0, keepdims=True)
            acc = zero
            for chunk in range(chunks):
                acc = fold(jnp.add, acc, jnp.exp2(score[pl.ds(chunk * CHUNK, CHUNK), :] - top))
            finish(block, top + jnp.log2(jnp.sum(acc, axis=0, keepdims=True)))
            return carry

        lax.fori_loop(0, blocks, exact, 0)

    for i in range(out.shape[0]):
        out[i] = out[i] + bound


def final_kernel(log_src, parts, yn, dual, xn, col_out, row_out):
    value = combine(parts, log_src) * (1.0 / SCALE) + yn[...]
    for i in range(col_out.shape[0]):
        col_out[i] = value
    row_out[...] = dual[...] * (1.0 / SCALE) + xn[...]


def params(mib):
    return pltpu.CompilerParams(vmem_limit_bytes=mib * 2**20)


def lse_pass(log_count, parts, prev, main, tail, rhs, copies):
    length, width = main.shape[0], rhs.shape[1]
    return pl.pallas_call(
        lambda *refs: pass_kernel(log_count, *refs),
        out_shape=(
            jax.ShapeDtypeStruct((copies, width // LANES, LANES), f32),
            jax.ShapeDtypeStruct((length // LANES, LANES), f32),
        ),
        in_specs=[vmem] * 5,
        out_specs=(vmem, vmem),
        scratch_shapes=[
            pltpu.VMEM((length, LANES), bf16),
            pltpu.VMEM((EDGE, width), bf16),
            pltpu.VMEM((length, WIDTH), f32),
        ],
        compiler_params=params(20),
    )(parts, prev, main, tail, rhs)


def gathered(value, axes):
    copies = jnp.broadcast_to(value[None], (lax.axis_size(axes),) + value.shape)
    return lax.all_to_all(copies, axes, 0, 0, tiled=True)


def exchanged(parts, axes):
    return lax.all_to_all(parts, axes, 0, 0, tiled=True)


ROW_GATHER = "x"
COL_GATHER = ("z", "yl")
ROW_PEERS = ("yh", "core", "x")
COL_PEERS = ("z", "yl")


def on_device(x_feat, y_feat):
    xg = gathered(x_feat, ROW_GATHER)
    yg = gathered(y_feat, COL_GATHER)
    rows, cols = xg.shape[0] * xg.shape[2], yg.shape[0] * yg.shape[2]
    row_peers, col_peers = lax.axis_size(ROW_PEERS), lax.axis_size(COL_PEERS)
    log_tgt = math.log2(cols * row_peers)
    log_src = math.log2(rows * col_peers)

    def side(cells):
        return [
            jax.ShapeDtypeStruct((cells, LANES), bf16),
            jax.ShapeDtypeStruct((cells, LANES), bf16),
            jax.ShapeDtypeStruct((3 * x_feat.shape[0], cells), bf16),
            jax.ShapeDtypeStruct((cells // LANES, LANES), f32),
        ]

    xm, xt, xr, xn, ym, yt, yr, yn, parts, before = pl.pallas_call(
        lambda *refs: prepare_kernel(log_src, *refs),
        out_shape=side(rows)
        + side(cols)
        + [
            jax.ShapeDtypeStruct((1, cols // LANES, LANES), f32),
            jax.ShapeDtypeStruct((rows // LANES, LANES), f32),
        ],
        in_specs=[vmem] * 2,
        out_specs=[vmem] * 10,
        compiler_params=params(20),
    )(xg, yg)
    dual_x = before
    for iteration in range(ITERS):
        sums, dual_y = lse_pass(log_src, parts, dual_x, ym, yt, xr, row_peers)
        parts = exchanged(sums, ROW_PEERS)
        sums, dual_x = lse_pass(log_tgt, parts, dual_y, xm, xt, yr, col_peers)
        parts = exchanged(sums, COL_PEERS)
    spread = lax.axis_size(ROW_GATHER)
    dual_col, dual_row = pl.pallas_call(
        lambda *refs: final_kernel(log_src, *refs),
        out_shape=(
            jax.ShapeDtypeStruct((spread, cols // LANES, LANES), f32),
            jax.ShapeDtypeStruct((rows // LANES, LANES), f32),
        ),
        in_specs=[vmem] * 4,
        out_specs=(vmem, vmem),
    )(parts, yn, dual_x, xn)
    own = x_feat.shape[1] // LANES
    dual_row = lax.dynamic_slice_in_dim(dual_row, lax.axis_index(ROW_GATHER) * own, own, 0)
    dual_col = exchanged(dual_col, ROW_GATHER)
    return dual_row.reshape(-1), dual_col.reshape(-1)


def solution(mesh):
    fine = Mesh(mesh.devices.reshape(2, 2, 4, 4, 2), ("yh", "core", "x", "z", "yl"))
    dev = ("x", "z", "yl")
    in_specs = (P(None, dev), P(None, ("yh", "core") + dev))
    out_specs = (P(dev), P(("yh", "core")))
    return jax.shard_map(
        on_device, mesh=fine, in_specs=in_specs, out_specs=out_specs, check_vma=False
    )
```

```python
import math

import jax
import jax.numpy as jnp
from jax import lax
from jax.experimental import pallas as pl
from jax.experimental.pallas import tpu as pltpu
from jax.sharding import Mesh
from jax.sharding import PartitionSpec as P

ITERS = 2
EPS = 0.5
LOG2E = 1.0 / math.log(2.0)
SCALE = LOG2E / EPS

LANES = 128
CHUNK = 256
WIDTH = 256
GROUP = 4
ACC_ROWS = 16
DUAL_LANE = 64
EDGE = 64
SMALLEST = 2.0**-80

f32 = jnp.float32
bf16 = jnp.bfloat16
vmem = pl.BlockSpec(memory_space=pltpu.VMEM)


def split2(value):
    high = value.astype(bf16)
    return high, (value - high.astype(f32)).astype(bf16)


def fold(op, acc, value):
    rows = acc.shape[0]
    for i in range(value.shape[0] // rows):
        acc = op(acc, value[i * rows : (i + 1) * rows])
    return acc


def prepare_block(value, at, main, tail, rhs, norm, scale):
    dim, cells = value.shape
    rows = cells // LANES
    square = jnp.sum(value * value, axis=0, keepdims=True)
    for q in range(rows):
        norm[pl.ds(at * rows + q, 1), :] = square[:, q * LANES : (q + 1) * LANES]
    high, low = split2(value * scale)
    here = pl.ds(pl.multiple_of(at * cells, cells), cells)
    rhs[0:dim, here] = high
    rhs[dim : 2 * dim, here] = low
    rhs[2 * dim : 3 * dim, here] = high
    main[here, :] = jnp.transpose(jnp.concatenate([high, high], axis=0))
    tail[here, :] = jnp.transpose(jnp.concatenate([low, jnp.zeros_like(low)], axis=0))


def prepare_kernel(log_src, index, *refs):
    xs, (y_ref, xm, xt, xr, xn, ym, yt, yr, yn, first, before) = refs[:-11], refs[-11:]
    for shift, x_ref in enumerate(xs):
        at = lax.rem(index[0] + len(xs) - shift, len(xs))
        prepare_block(x_ref[...], at, xm, xt, xr, xn, 2.0 * SCALE)
    for at in range(y_ref.shape[0]):
        prepare_block(y_ref[at], at, ym, yt, yr, yn, 1.0)
    first[0] = log_src + SCALE * yn[...]
    before[...] = log_src - SCALE * xn[...]


def combine(parts, log_count):
    peak = parts[0]
    for i in range(1, parts.shape[0]):
        peak = jnp.maximum(peak, parts[i])
    total = jnp.exp2(parts[0] - peak)
    for i in range(1, parts.shape[0]):
        total = total + jnp.exp2(parts[i] - peak)
    return log_count - (peak + jnp.log2(total))


def split3(value):
    high = value.astype(bf16).astype(f32)
    mid = (value - high).astype(bf16).astype(f32)
    return high, mid, value - high - mid


def placed(parts, row, height, first):
    place = lax.broadcasted_iota(jnp.int32, (height, LANES), 0)
    value = jnp.zeros((height, LANES), f32)
    for i, part in enumerate(parts):
        value = jnp.where(place == first + i, part[row : row + 1], value)
    return value


def pass_kernel(log_count, parts, prev, main, tail, rhs, out, dual_out, full, edge, score):
    length, width = main.shape[0], rhs.shape[1]
    dual = combine(parts, log_count)
    dual_out[...] = dual
    bound = log_count - prev[...]
    duals, bounds = split3(dual), split3(-bound)
    place = lax.broadcasted_iota(jnp.int32, (LANES, LANES), 0)
    for k in range(length // LANES):
        here = pl.ds(k * LANES, LANES)
        rows = placed(duals, k, LANES, DUAL_LANE)
        rows = jnp.where((place >= DUAL_LANE + 3) & (place < DUAL_LANE + 6), 1.0, rows)
        full[here, :] = (tail[here, :].astype(f32) + jnp.transpose(rows)).astype(bf16)
    place = lax.broadcasted_iota(jnp.int32, (EDGE, LANES), 0)
    for k in range(width // LANES):
        rows = jnp.where(place < 3, 1.0, placed(bounds, k, EDGE, 3))
        edge[:, pl.ds(k * LANES, LANES)] = rows.astype(bf16)

    def scores(block, chunk):
        here = pl.ds(chunk * CHUNK, CHUNK)
        lhs = jnp.concatenate([main[here, :], full[here, :]], axis=1)
        cols = pl.ds(pl.multiple_of(block * WIDTH, WIDTH), WIDTH)
        weight = jnp.concatenate([rhs[:, cols], edge[:, cols]], axis=0)
        return jnp.dot(lhs, weight, preferred_element_type=f32)

    def finish(block, value):
        for q in range(WIDTH // LANES):
            row = block * (WIDTH // LANES) + q
            piece = value[:, q * LANES : (q + 1) * LANES][None]
            out[:, pl.ds(row, 1), :] = jnp.broadcast_to(piece, (out.shape[0], 1, LANES))

    chunks, blocks = length // CHUNK, width // WIDTH
    zero = jnp.zeros((ACC_ROWS, WIDTH), f32)

    def step(group, least):
        for t in range(GROUP):
            block = group * GROUP + t
            acc = zero
            for chunk in range(chunks):
                acc = fold(jnp.add, acc, jnp.exp2(scores(block, chunk)))
            total = jnp.sum(acc, axis=0, keepdims=True)
            least = jnp.minimum(least, total)
            finish(block, jnp.log2(total))
        return least

    least = lax.fori_loop(0, blocks // GROUP, step, jnp.full((1, WIDTH), 1.0, f32))

    @pl.when(jnp.min(least) < SMALLEST)
    def _():
        def exact(block, carry):
            peak = jnp.full((ACC_ROWS, WIDTH), -jnp.inf, f32)
            for chunk in range(chunks):
                value = scores(block, chunk)
                score[pl.ds(chunk * CHUNK, CHUNK), :] = value
                peak = fold(jnp.maximum, peak, value)
            top = jnp.max(peak, axis=0, keepdims=True)
            acc = zero
            for chunk in range(chunks):
                acc = fold(jnp.add, acc, jnp.exp2(score[pl.ds(chunk * CHUNK, CHUNK), :] - top))
            finish(block, top + jnp.log2(jnp.sum(acc, axis=0, keepdims=True)))
            return carry

        lax.fori_loop(0, blocks, exact, 0)

    for i in range(out.shape[0]):
        out[i] = out[i] + bound


def final_kernel(log_src, parts, yn, dual, xn, col_out, row_out):
    value = combine(parts, log_src) * (1.0 / SCALE) + yn[...]
    for i in range(col_out.shape[0]):
        col_out[i] = value
    row_out[...] = dual[...] * (1.0 / SCALE) + xn[...]


def params(mib):
    return pltpu.CompilerParams(vmem_limit_bytes=mib * 2**20)


def lse_pass(log_count, parts, prev, main, tail, rhs, copies):
    length, width = main.shape[0], rhs.shape[1]
    return pl.pallas_call(
        lambda *refs: pass_kernel(log_count, *refs),
        out_shape=(
            jax.ShapeDtypeStruct((copies, width // LANES, LANES), f32),
            jax.ShapeDtypeStruct((length // LANES, LANES), f32),
        ),
        in_specs=[vmem] * 5,
        out_specs=(vmem, vmem),
        scratch_shapes=[
            pltpu.VMEM((length, LANES), bf16),
            pltpu.VMEM((EDGE, width), bf16),
            pltpu.VMEM((length, WIDTH), f32),
        ],
        compiler_params=params(20),
    )(parts, prev, main, tail, rhs)


def gathered(value, axes):
    copies = jnp.broadcast_to(value[None], (lax.axis_size(axes),) + value.shape)
    return lax.all_to_all(copies, axes, 0, 0, tiled=True)


def exchanged(parts, axes):
    return lax.all_to_all(parts, axes, 0, 0, tiled=True)


ROW_GATHER = "x"
COL_GATHER = ("z", "yl")
ROW_PEERS = ("yh", "core", "x")
COL_PEERS = ("z", "yl")


def on_device(x_feat, y_feat):
    ring = lax.axis_size(ROW_GATHER)
    blocks = [x_feat]
    for shift in range(1, ring):
        pairs = [(i, (i + shift) % ring) for i in range(ring)]
        blocks.append(lax.ppermute(x_feat, ROW_GATHER, pairs))
    yg = gathered(y_feat, COL_GATHER)
    rows, cols = ring * x_feat.shape[1], yg.shape[0] * yg.shape[2]
    row_peers, col_peers = lax.axis_size(ROW_PEERS), lax.axis_size(COL_PEERS)
    log_tgt = math.log2(cols * row_peers)
    log_src = math.log2(rows * col_peers)

    def side(cells):
        return [
            jax.ShapeDtypeStruct((cells, LANES), bf16),
            jax.ShapeDtypeStruct((cells, LANES), bf16),
            jax.ShapeDtypeStruct((3 * x_feat.shape[0], cells), bf16),
            jax.ShapeDtypeStruct((cells // LANES, LANES), f32),
        ]

    xm, xt, xr, xn, ym, yt, yr, yn, parts, before = pl.pallas_call(
        lambda *refs: prepare_kernel(log_src, *refs),
        out_shape=side(rows)
        + side(cols)
        + [
            jax.ShapeDtypeStruct((1, cols // LANES, LANES), f32),
            jax.ShapeDtypeStruct((rows // LANES, LANES), f32),
        ],
        in_specs=[pl.BlockSpec(memory_space=pltpu.SMEM)] + [vmem] * (ring + 1),
        out_specs=[vmem] * 10,
        compiler_params=params(20),
    )(lax.axis_index(ROW_GATHER).reshape(1), *blocks, yg)
    dual_x = before
    for iteration in range(ITERS):
        sums, dual_y = lse_pass(log_src, parts, dual_x, ym, yt, xr, row_peers)
        parts = exchanged(sums, ROW_PEERS)
        sums, dual_x = lse_pass(log_tgt, parts, dual_y, xm, xt, yr, col_peers)
        parts = exchanged(sums, COL_PEERS)
    dual_col, dual_row = pl.pallas_call(
        lambda *refs: final_kernel(log_src, *refs),
        out_shape=(
            jax.ShapeDtypeStruct((ring, cols // LANES, LANES), f32),
            jax.ShapeDtypeStruct((rows // LANES, LANES), f32),
        ),
        in_specs=[vmem] * 4,
        out_specs=(vmem, vmem),
    )(parts, yn, dual_x, xn)
    own = x_feat.shape[1] // LANES
    dual_row = lax.dynamic_slice_in_dim(dual_row, lax.axis_index(ROW_GATHER) * own, own, 0)
    dual_col = exchanged(dual_col, ROW_GATHER)
    return dual_row.reshape(-1), dual_col.reshape(-1)


def solution(mesh):
    fine = Mesh(mesh.devices.reshape(2, 2, 4, 4, 2), ("yh", "core", "x", "z", "yl"))
    dev = ("x", "z", "yl")
    in_specs = (P(None, dev), P(None, ("yh", "core") + dev))
    out_specs = (P(dev), P(("yh", "core")))
    return jax.shard_map(
        on_device, mesh=fine, in_specs=in_specs, out_specs=out_specs, check_vma=False
    )
```

```python
import math

import jax
import jax.numpy as jnp
from jax import lax
from jax.experimental import pallas as pl
from jax.experimental.pallas import tpu as pltpu
from jax.sharding import Mesh
from jax.sharding import PartitionSpec as P

ITERS = 2
EPS = 0.5
LOG2E = 1.0 / math.log(2.0)
SCALE = LOG2E / EPS

LANES = 128
CHUNK = 256
WIDTH = 256
GROUP = 4
ACC_ROWS = 16
DUAL_LANE = 64
EDGE = 64
SMALLEST = 2.0**-80

f32 = jnp.float32
bf16 = jnp.bfloat16
vmem = pl.BlockSpec(memory_space=pltpu.VMEM)
smem = pl.BlockSpec(memory_space=pltpu.SMEM)


def split2(value):
    high = value.astype(bf16)
    return high, (value - high.astype(f32)).astype(bf16)


def fold(op, acc, value):
    rows = acc.shape[0]
    for i in range(value.shape[0] // rows):
        acc = op(acc, value[i * rows : (i + 1) * rows])
    return acc


def prepare_block(value, at, main, tail, rhs, norm, scale):
    dim, cells = value.shape
    rows = cells // LANES
    square = jnp.sum(value * value, axis=0, keepdims=True)
    for q in range(rows):
        norm[pl.ds(at * rows + q, 1), :] = square[:, q * LANES : (q + 1) * LANES]
    high, low = split2(value * scale)
    here = pl.ds(pl.multiple_of(at * cells, cells), cells)
    rhs[0:dim, here] = high
    rhs[dim : 2 * dim, here] = low
    rhs[2 * dim : 3 * dim, here] = high
    main[here, :] = jnp.transpose(jnp.concatenate([high, high], axis=0))
    tail[here, :] = jnp.transpose(jnp.concatenate([low, jnp.zeros_like(low)], axis=0))


def prepare_kernel(log_src, index, *refs):
    xs, (y_ref, xm, xt, xr, xn, ym, yt, yr, yn, first, before) = refs[:-11], refs[-11:]
    for shift, x_ref in enumerate(xs):
        at = lax.rem(index[0] + len(xs) - shift, len(xs))
        prepare_block(x_ref[...], at, xm, xt, xr, xn, 2.0 * SCALE)
    for at in range(y_ref.shape[0]):
        prepare_block(y_ref[at], at, ym, yt, yr, yn, 1.0)
    first[0] = log_src + SCALE * yn[...]
    before[...] = log_src - SCALE * xn[...]


def combine(parts, log_count):
    peak = parts[0]
    for i in range(1, parts.shape[0]):
        peak = jnp.maximum(peak, parts[i])
    total = jnp.exp2(parts[0] - peak)
    for i in range(1, parts.shape[0]):
        total = total + jnp.exp2(parts[i] - peak)
    return log_count - (peak + jnp.log2(total))


def split3(value):
    high = value.astype(bf16).astype(f32)
    mid = (value - high).astype(bf16).astype(f32)
    return high, mid, value - high - mid


def placed(parts, row, height, first):
    place = lax.broadcasted_iota(jnp.int32, (height, LANES), 0)
    value = jnp.zeros((height, LANES), f32)
    for i, part in enumerate(parts):
        value = jnp.where(place == first + i, part[row : row + 1], value)
    return value


def pass_kernel(log_count, parts, prev, norm, main, tail, rhs, out, dual_out, full, edge, score):
    length, width = main.shape[0], rhs.shape[1]
    dual = combine(parts, log_count)
    dual_out[...] = dual
    bound = log_count - prev[...]
    duals, bounds = split3(dual), split3(-bound)
    place = lax.broadcasted_iota(jnp.int32, (LANES, LANES), 0)
    for k in range(length // LANES):
        here = pl.ds(k * LANES, LANES)
        rows = placed(duals, k, LANES, DUAL_LANE)
        rows = jnp.where((place >= DUAL_LANE + 3) & (place < DUAL_LANE + 6), 1.0, rows)
        full[here, :] = (tail[here, :].astype(f32) + jnp.transpose(rows)).astype(bf16)
    place = lax.broadcasted_iota(jnp.int32, (EDGE, LANES), 0)
    for k in range(width // LANES):
        rows = jnp.where(place < 3, 1.0, placed(bounds, k, EDGE, 3))
        edge[:, pl.ds(k * LANES, LANES)] = rows.astype(bf16)

    def scores(block, chunk):
        here = pl.ds(chunk * CHUNK, CHUNK)
        lhs = jnp.concatenate([main[here, :], full[here, :]], axis=1)
        cols = pl.ds(pl.multiple_of(block * WIDTH, WIDTH), WIDTH)
        weight = jnp.concatenate([rhs[:, cols], edge[:, cols]], axis=0)
        return jnp.dot(lhs, weight, preferred_element_type=f32)

    def finish(block, value):
        for q in range(WIDTH // LANES):
            row = block * (WIDTH // LANES) + q
            piece = value[:, q * LANES : (q + 1) * LANES][None]
            out[:, pl.ds(row, 1), :] = jnp.broadcast_to(piece, (out.shape[0], 1, LANES))

    chunks, blocks = length // CHUNK, width // WIDTH
    zero = jnp.zeros((ACC_ROWS, WIDTH), f32)

    def step(group, least):
        for t in range(GROUP):
            block = group * GROUP + t
            acc = zero
            for chunk in range(chunks):
                acc = fold(jnp.add, acc, jnp.exp2(scores(block, chunk)))
            total = jnp.sum(acc, axis=0, keepdims=True)
            least = jnp.minimum(least, total)
            finish(block, jnp.log2(total))
        return least

    least = lax.fori_loop(0, blocks // GROUP, step, jnp.full((1, WIDTH), 1.0, f32))

    @pl.when(jnp.min(least) < SMALLEST)
    def _():
        def exact(block, carry):
            peak = jnp.full((ACC_ROWS, WIDTH), -jnp.inf, f32)
            for chunk in range(chunks):
                value = scores(block, chunk)
                score[pl.ds(chunk * CHUNK, CHUNK), :] = value
                peak = fold(jnp.maximum, peak, value)
            top = jnp.max(peak, axis=0, keepdims=True)
            acc = zero
            for chunk in range(chunks):
                acc = fold(jnp.add, acc, jnp.exp2(score[pl.ds(chunk * CHUNK, CHUNK), :] - top))
            finish(block, top + jnp.log2(jnp.sum(acc, axis=0, keepdims=True)))
            return carry

        lax.fori_loop(0, blocks, exact, 0)

    offset = bound if norm is None else bound - SCALE * norm[...]
    for i in range(out.shape[0]):
        out[i] = out[i] + offset


def final_kernel(log_src, index, parts, dual, xn, col_out, row_out):
    blocks = col_out.shape[0]
    peers = parts.shape[0] // blocks
    for block in range(blocks):
        col_out[block] = combine(parts[block * peers : (block + 1) * peers], log_src) * (1.0 / SCALE)
    rows = row_out.shape[0]
    own = pl.ds(pl.multiple_of(index[0] * rows, rows), rows)
    row_out[...] = dual[own, :] * (1.0 / SCALE) + xn[own, :]


def params(mib):
    return pltpu.CompilerParams(vmem_limit_bytes=mib * 2**20)


def lse_pass(log_count, parts, prev, main, tail, rhs, copies, norm=None):
    length, width = main.shape[0], rhs.shape[1]
    norms = [] if norm is None else [norm]

    def kernel(parts, prev, *refs):
        at = len(norms)
        pass_kernel(log_count, parts, prev, refs[0] if at else None, *refs[at:])

    return pl.pallas_call(
        kernel,
        out_shape=(
            jax.ShapeDtypeStruct((copies, width // LANES, LANES), f32),
            jax.ShapeDtypeStruct((length // LANES, LANES), f32),
        ),
        in_specs=[vmem] * (5 + len(norms)),
        out_specs=(vmem, vmem),
        scratch_shapes=[
            pltpu.VMEM((length, LANES), bf16),
            pltpu.VMEM((EDGE, width), bf16),
            pltpu.VMEM((length, WIDTH), f32),
        ],
        compiler_params=params(12),
    )(parts, prev, *norms, main, tail, rhs)


def gathered(value, axes):
    copies = jnp.broadcast_to(value[None], (lax.axis_size(axes),) + value.shape)
    return lax.all_to_all(copies, axes, 0, 0, tiled=True)


def exchanged(parts, axes):
    return lax.all_to_all(parts, axes, 0, 0, tiled=True)


ROW_GATHER = "x"
COL_GATHER = ("z", "yl")
ROW_PEERS = ("yh", "core", "x")
COL_PEERS = ("z", "yl")
DEV = ("x", "z", "yl")


def on_device(x_feat, y_feat):
    ring = lax.axis_size(ROW_GATHER)
    index = lax.axis_index(ROW_GATHER).reshape(1)
    blocks = [x_feat]
    for shift in range(1, ring):
        pairs = [(i, (i + shift) % ring) for i in range(ring)]
        blocks.append(lax.ppermute(x_feat, ROW_GATHER, pairs))
    yg = gathered(y_feat, COL_GATHER)
    rows, cols = ring * x_feat.shape[1], yg.shape[0] * yg.shape[2]
    row_peers, col_peers = lax.axis_size(ROW_PEERS), lax.axis_size(COL_PEERS)
    log_tgt = math.log2(cols * row_peers)
    log_src = math.log2(rows * col_peers)

    def side(cells):
        return [
            jax.ShapeDtypeStruct((cells, LANES), bf16),
            jax.ShapeDtypeStruct((cells, LANES), bf16),
            jax.ShapeDtypeStruct((3 * x_feat.shape[0], cells), bf16),
            jax.ShapeDtypeStruct((cells // LANES, LANES), f32),
        ]

    xm, xt, xr, xn, ym, yt, yr, yn, parts, before = pl.pallas_call(
        lambda *refs: prepare_kernel(log_src, *refs),
        out_shape=side(rows)
        + side(cols)
        + [
            jax.ShapeDtypeStruct((1, cols // LANES, LANES), f32),
            jax.ShapeDtypeStruct((rows // LANES, LANES), f32),
        ],
        in_specs=[smem] + [vmem] * (ring + 1),
        out_specs=[vmem] * 10,
        compiler_params=params(20),
    )(index, *blocks, yg)
    dual_x = before
    for iteration in range(ITERS):
        sums, dual_y = lse_pass(log_src, parts, dual_x, ym, yt, xr, row_peers)
        parts = exchanged(sums, ROW_PEERS)
        if iteration < ITERS - 1:
            sums, dual_x = lse_pass(log_tgt, parts, dual_y, xm, xt, yr, col_peers)
            parts = exchanged(sums, COL_PEERS)
    sums, dual_x = lse_pass(log_tgt, parts, dual_y, xm, xt, yr, lax.axis_size(DEV), yn)
    parts = exchanged(sums, DEV)
    dual_col, dual_row = pl.pallas_call(
        lambda *refs: final_kernel(log_src, *refs),
        out_shape=(
            jax.ShapeDtypeStruct((ring, cols // LANES, LANES), f32),
            jax.ShapeDtypeStruct((x_feat.shape[1] // LANES, LANES), f32),
        ),
        in_specs=[smem] + [vmem] * 3,
        out_specs=(vmem, vmem),
        compiler_params=params(4),
    )(index, parts, dual_x, xn)
    return dual_row.reshape(-1), dual_col.reshape(-1)


def solution(mesh):
    fine = Mesh(mesh.devices.reshape(2, 2, 4, 4, 2), ("yh", "core", "x", "z", "yl"))
    in_specs = (P(None, DEV), P(None, ("yh", "core") + DEV))
    out_specs = (P(DEV), P(("yh", "core")))
    return jax.shard_map(
        on_device, mesh=fine, in_specs=in_specs, out_specs=out_specs, check_vma=False
    )
```

```python
import math

import jax
import jax.numpy as jnp
from jax import lax
from jax.experimental import pallas as pl
from jax.experimental.pallas import tpu as pltpu
from jax.sharding import Mesh
from jax.sharding import PartitionSpec as P

ITERS = 2
EPS = 0.5
LOG2E = 1.0 / math.log(2.0)
SCALE = LOG2E / EPS

LANES = 128
CHUNK = 256
WIDTH = 256
GROUP = 4
ACC_ROWS = 16
DUAL_LANE = 64
EDGE = 64
SMALLEST = 2.0**-80

f32 = jnp.float32
bf16 = jnp.bfloat16
vmem = pl.BlockSpec(memory_space=pltpu.VMEM)
smem = pl.BlockSpec(memory_space=pltpu.SMEM)


def split2(value):
    high = value.astype(bf16)
    return high, (value - high.astype(f32)).astype(bf16)


def fold(op, acc, value):
    rows = acc.shape[0]
    for i in range(value.shape[0] // rows):
        acc = op(acc, value[i * rows : (i + 1) * rows])
    return acc


def prepare_block(value, at, main, tail, rhs, norm, scale):
    dim, cells = value.shape
    rows = cells // LANES
    square = jnp.sum(value * value, axis=0, keepdims=True)
    for q in range(rows):
        norm[pl.ds(at * rows + q, 1), :] = square[:, q * LANES : (q + 1) * LANES]
    high, low = split2(value * scale)
    here = pl.ds(pl.multiple_of(at * cells, cells), cells)
    rhs[0:dim, here] = high
    rhs[dim : 2 * dim, here] = low
    rhs[2 * dim : 3 * dim, here] = high
    main[here, :] = jnp.transpose(jnp.concatenate([high, high], axis=0))
    tail[here, :] = jnp.transpose(jnp.concatenate([low, jnp.zeros_like(low)], axis=0))


def prepare_kernel(log_src, index, *refs):
    xs, (y_ref, xm, xt, xr, xn, ym, yt, yr, yn, first, before) = refs[:-11], refs[-11:]
    for shift, x_ref in enumerate(xs):
        at = lax.rem(index[0] + len(xs) - shift, len(xs))
        prepare_block(x_ref[...], at, xm, xt, xr, xn, 2.0 * SCALE)
    for at in range(y_ref.shape[0]):
        prepare_block(y_ref[at], at, ym, yt, yr, yn, 1.0)
    first[0] = log_src + SCALE * yn[...]
    before[...] = log_src - SCALE * xn[...]


def combine(parts, log_count):
    peak = parts[0]
    for i in range(1, parts.shape[0]):
        peak = jnp.maximum(peak, parts[i])
    total = jnp.exp2(parts[0] - peak)
    for i in range(1, parts.shape[0]):
        total = total + jnp.exp2(parts[i] - peak)
    return log_count - (peak + jnp.log2(total))


def split3(value):
    high = value.astype(bf16).astype(f32)
    mid = (value - high).astype(bf16).astype(f32)
    return high, mid, value - high - mid


def placed(parts, row, height, first):
    place = lax.broadcasted_iota(jnp.int32, (height, LANES), 0)
    value = jnp.zeros((height, LANES), f32)
    for i, part in enumerate(parts):
        value = jnp.where(place == first + i, part[row : row + 1], value)
    return value


def pass_kernel(log_count, parts, prev, norm, main, tail, rhs, out, dual_out, full, edge, score):
    length, width = main.shape[0], rhs.shape[1]
    dual = combine(parts, log_count)
    dual_out[...] = dual
    bound = log_count - prev[...]
    duals, bounds = split3(dual), split3(-bound)
    place = lax.broadcasted_iota(jnp.int32, (LANES, LANES), 0)
    for k in range(length // LANES):
        here = pl.ds(k * LANES, LANES)
        rows = placed(duals, k, LANES, DUAL_LANE)
        rows = jnp.where((place >= DUAL_LANE + 3) & (place < DUAL_LANE + 6), 1.0, rows)
        full[here, :] = (tail[here, :].astype(f32) + jnp.transpose(rows)).astype(bf16)
    place = lax.broadcasted_iota(jnp.int32, (EDGE, LANES), 0)
    for k in range(width // LANES):
        rows = jnp.where(place < 3, 1.0, placed(bounds, k, EDGE, 3))
        edge[:, pl.ds(k * LANES, LANES)] = rows.astype(bf16)

    def scores(block, chunk):
        here = pl.ds(chunk * CHUNK, CHUNK)
        lhs = jnp.concatenate([main[here, :], full[here, :]], axis=1)
        cols = pl.ds(pl.multiple_of(block * WIDTH, WIDTH), WIDTH)
        weight = jnp.concatenate([rhs[:, cols], edge[:, cols]], axis=0)
        return jnp.dot(lhs, weight, preferred_element_type=f32)

    def finish(block, value):
        for q in range(WIDTH // LANES):
            row = block * (WIDTH // LANES) + q
            piece = value[:, q * LANES : (q + 1) * LANES][None]
            out[:, pl.ds(row, 1), :] = jnp.broadcast_to(piece, (out.shape[0], 1, LANES))

    chunks, blocks = length // CHUNK, width // WIDTH
    zero = jnp.zeros((ACC_ROWS, WIDTH), f32)

    def step(group, least):
        for t in range(GROUP):
            block = group * GROUP + t
            acc = zero
            for chunk in range(chunks):
                acc = fold(jnp.add, acc, jnp.exp2(scores(block, chunk)))
            total = jnp.sum(acc, axis=0, keepdims=True)
            least = jnp.minimum(least, total)
            finish(block, jnp.log2(total))
        return least

    least = lax.fori_loop(0, blocks // GROUP, step, jnp.full((1, WIDTH), 1.0, f32))

    @pl.when(jnp.min(least) < SMALLEST)
    def _():
        def exact(block, carry):
            peak = jnp.full((ACC_ROWS, WIDTH), -jnp.inf, f32)
            for chunk in range(chunks):
                value = scores(block, chunk)
                score[pl.ds(chunk * CHUNK, CHUNK), :] = value
                peak = fold(jnp.maximum, peak, value)
            top = jnp.max(peak, axis=0, keepdims=True)
            acc = zero
            for chunk in range(chunks):
                acc = fold(jnp.add, acc, jnp.exp2(score[pl.ds(chunk * CHUNK, CHUNK), :] - top))
            finish(block, top + jnp.log2(jnp.sum(acc, axis=0, keepdims=True)))
            return carry

        lax.fori_loop(0, blocks, exact, 0)

    offset = bound if norm is None else bound - SCALE * norm[...]
    for i in range(out.shape[0]):
        out[i] = out[i] + offset


def final_kernel(log_src, index, parts, dual, xn, col_out, row_out):
    blocks = col_out.shape[0]
    peers = parts.shape[0] // blocks
    for block in range(blocks):
        col_out[block] = combine(parts[block * peers : (block + 1) * peers], log_src) * (1.0 / SCALE)
    rows = row_out.shape[0]
    own = pl.ds(pl.multiple_of(index[0] * rows, rows), rows)
    row_out[...] = dual[own, :] * (1.0 / SCALE) + xn[own, :]


def params(mib):
    return pltpu.CompilerParams(vmem_limit_bytes=mib * 2**20)


def lse_pass(log_count, parts, prev, main, tail, rhs, copies, norm=None):
    length, width = main.shape[0], rhs.shape[1]
    norms = [] if norm is None else [norm]

    def kernel(parts, prev, *refs):
        at = len(norms)
        pass_kernel(log_count, parts, prev, refs[0] if at else None, *refs[at:])

    return pl.pallas_call(
        kernel,
        out_shape=(
            jax.ShapeDtypeStruct((copies, width // LANES, LANES), f32),
            jax.ShapeDtypeStruct((length // LANES, LANES), f32),
        ),
        in_specs=[vmem] * (5 + len(norms)),
        out_specs=(vmem, vmem),
        scratch_shapes=[
            pltpu.VMEM((length, LANES), bf16),
            pltpu.VMEM((EDGE, width), bf16),
            pltpu.VMEM((length, WIDTH), f32),
        ],
        compiler_params=params(9),
    )(parts, prev, *norms, main, tail, rhs)


def repeat_kernel(value, out):
    for i in range(out.shape[0]):
        out[i] = value[...]


def gathered(value, axes):
    copies = pl.pallas_call(
        repeat_kernel,
        out_shape=jax.ShapeDtypeStruct((lax.axis_size(axes),) + value.shape, value.dtype),
        in_specs=[vmem],
        out_specs=vmem,
        compiler_params=params(4),
    )(value)
    return lax.all_to_all(copies, axes, 0, 0, tiled=True)


def exchanged(parts, axes):
    return lax.all_to_all(parts, axes, 0, 0, tiled=True)


ROW_GATHER = "x"
COL_GATHER = ("z", "yl")
ROW_PEERS = ("yh", "core", "x")
COL_PEERS = ("z", "yl")
DEV = ("x", "z", "yl")


def on_device(x_feat, y_feat):
    ring = lax.axis_size(ROW_GATHER)
    index = lax.axis_index(ROW_GATHER).reshape(1)
    blocks = [x_feat]
    for shift in range(1, ring):
        pairs = [(i, (i + shift) % ring) for i in range(ring)]
        blocks.append(lax.ppermute(x_feat, ROW_GATHER, pairs))
    yg = gathered(y_feat, COL_GATHER)
    rows, cols = ring * x_feat.shape[1], yg.shape[0] * yg.shape[2]
    row_peers, col_peers = lax.axis_size(ROW_PEERS), lax.axis_size(COL_PEERS)
    log_tgt = math.log2(cols * row_peers)
    log_src = math.log2(rows * col_peers)

    def side(cells):
        return [
            jax.ShapeDtypeStruct((cells, LANES), bf16),
            jax.ShapeDtypeStruct((cells, LANES), bf16),
            jax.ShapeDtypeStruct((3 * x_feat.shape[0], cells), bf16),
            jax.ShapeDtypeStruct((cells // LANES, LANES), f32),
        ]

    xm, xt, xr, xn, ym, yt, yr, yn, parts, before = pl.pallas_call(
        lambda *refs: prepare_kernel(log_src, *refs),
        out_shape=side(rows)
        + side(cols)
        + [
            jax.ShapeDtypeStruct((1, cols // LANES, LANES), f32),
            jax.ShapeDtypeStruct((rows // LANES, LANES), f32),
        ],
        in_specs=[smem] + [vmem] * (ring + 1),
        out_specs=[vmem] * 10,
        compiler_params=params(9),
    )(index, *blocks, yg)
    dual_x = before
    for iteration in range(ITERS):
        sums, dual_y = lse_pass(log_src, parts, dual_x, ym, yt, xr, row_peers)
        parts = exchanged(sums, ROW_PEERS)
        if iteration < ITERS - 1:
            sums, dual_x = lse_pass(log_tgt, parts, dual_y, xm, xt, yr, col_peers)
            parts = exchanged(sums, COL_PEERS)
    sums, dual_x = lse_pass(log_tgt, parts, dual_y, xm, xt, yr, lax.axis_size(DEV), yn)
    parts = exchanged(sums, DEV)
    dual_col, dual_row = pl.pallas_call(
        lambda *refs: final_kernel(log_src, *refs),
        out_shape=(
            jax.ShapeDtypeStruct((ring, cols // LANES, LANES), f32),
            jax.ShapeDtypeStruct((x_feat.shape[1] // LANES, LANES), f32),
        ),
        in_specs=[smem] + [vmem] * 3,
        out_specs=(vmem, vmem),
        compiler_params=params(4),
    )(index, parts, dual_x, xn)
    return dual_row.reshape(-1), dual_col.reshape(-1)


def solution(mesh):
    fine = Mesh(mesh.devices.reshape(2, 2, 4, 4, 2), ("yh", "core", "x", "z", "yl"))
    in_specs = (P(None, DEV), P(None, ("yh", "core") + DEV))
    out_specs = (P(DEV), P(("yh", "core")))
    return jax.shard_map(
        on_device, mesh=fine, in_specs=in_specs, out_specs=out_specs, check_vma=False
    )
```

```python
import math

import jax
import jax.numpy as jnp
from jax import lax
from jax.experimental import pallas as pl
from jax.experimental.pallas import tpu as pltpu
from jax.sharding import Mesh
from jax.sharding import PartitionSpec as P

ITERS = 2
EPS = 0.5
LOG2E = 1.0 / math.log(2.0)
SCALE = LOG2E / EPS

LANES = 128
CHUNK = 256
WIDTH = 256
GROUP = 4
ACC_ROWS = 16
DUAL_LANE = 64
EDGE = 64
SUBLANES = 8
SMALLEST = 2.0**-80

f32 = jnp.float32
bf16 = jnp.bfloat16
vmem = pl.BlockSpec(memory_space=pltpu.VMEM)
smem = pl.BlockSpec(memory_space=pltpu.SMEM)


def split2(value):
    high = value.astype(bf16)
    return high, (value - high.astype(f32)).astype(bf16)


def fold(op, acc, value):
    rows = acc.shape[0]
    for i in range(value.shape[0] // rows):
        acc = op(acc, value[i * rows : (i + 1) * rows])
    return acc


def prepare_block(value, at, main, tail, rhs, norm, scale):
    dim, cells = value.shape
    rows = cells // LANES
    square = jnp.sum(value * value, axis=0, keepdims=True)
    for q in range(rows):
        norm[pl.ds(at * rows + q, 1), :] = square[:, q * LANES : (q + 1) * LANES]
    high, low = split2(value * scale)
    here = pl.ds(pl.multiple_of(at * cells, cells), cells)
    rhs[0:dim, here] = high
    rhs[dim : 2 * dim, here] = low
    rhs[2 * dim : 3 * dim, here] = high
    main[here, :] = jnp.transpose(jnp.concatenate([high, high], axis=0))
    tail[here, :] = jnp.transpose(jnp.concatenate([low, jnp.zeros_like(low)], axis=0))


def combine(parts, log_count):
    peak = parts[0]
    for i in range(1, parts.shape[0]):
        peak = jnp.maximum(peak, parts[i])
    total = jnp.exp2(parts[0] - peak)
    for i in range(1, parts.shape[0]):
        total = total + jnp.exp2(parts[i] - peak)
    return log_count - (peak + jnp.log2(total))


def split3(value):
    high = value.astype(bf16).astype(f32)
    mid = (value - high).astype(bf16).astype(f32)
    return high, mid, value - high - mid


def stacked(parts, row, ones):
    place = lax.broadcasted_iota(jnp.int32, (SUBLANES, LANES), 0)
    value = jnp.where(place < 6, 1.0, 0.0)
    for i, part in enumerate(parts):
        value = jnp.where(place == (3 - ones) + i, part[row : row + 1], value)
    return value


def fill_duals(dual, tail, full):
    parts = split3(dual)
    before = jnp.zeros((DUAL_LANE, LANES), f32)
    after = jnp.zeros((LANES - DUAL_LANE - SUBLANES, LANES), f32)
    for k in range(dual.shape[0]):
        here = pl.ds(k * LANES, LANES)
        rows = jnp.concatenate([before, stacked(parts, k, 3), after], axis=0)
        full[here, :] = (tail[here, :].astype(f32) + jnp.transpose(rows)).astype(bf16)


def fill_bounds(bound, edge, start):
    parts = split3(-bound)
    cells = bound.shape[0] * LANES
    edge[2 * SUBLANES :, pl.ds(start, cells)] = jnp.zeros((EDGE - 2 * SUBLANES, cells), bf16)
    for k in range(bound.shape[0]):
        rows = jnp.concatenate([stacked(parts, k, 0), jnp.zeros((SUBLANES, LANES), f32)], axis=0)
        edge[0 : 2 * SUBLANES, pl.ds(start + k * LANES, LANES)] = rows.astype(bf16)


def column_logs(main, full, rhs, edge, logs, partial, low, count):
    chunks = main.shape[0] // CHUNK
    rows_of = WIDTH // LANES

    def scores(block, chunk):
        here = pl.ds(chunk * CHUNK, CHUNK)
        if not isinstance(chunk, int):
            here = pl.ds(pl.multiple_of(chunk * CHUNK, CHUNK), CHUNK)
        cols = pl.ds(pl.multiple_of(block * WIDTH, WIDTH), WIDTH)
        lhs = jnp.concatenate([main[here, :], full[here, :]], axis=1)
        weight = jnp.concatenate([rhs[:, cols], edge[:, cols]], axis=0)
        return jnp.dot(lhs, weight, preferred_element_type=f32)

    def finish(block, value):
        for q in range(rows_of):
            logs[pl.ds(block * rows_of + q, 1), :] = value[:, q * LANES : (q + 1) * LANES]

    zero = jnp.zeros((ACC_ROWS, WIDTH), f32)

    def step(group, carry):
        for t in range(GROUP):
            block, acc = group * GROUP + t, zero
            for chunk in range(chunks):
                acc = fold(jnp.add, acc, jnp.exp2(scores(low + block, chunk)))
            here = pl.ds(pl.multiple_of(block * SUBLANES, SUBLANES), SUBLANES)
            partial[here, :] = fold(jnp.add, acc[:SUBLANES], acc[SUBLANES:])
        return carry

    lax.fori_loop(0, count // GROUP, step, 0)
    least = jnp.full((1, WIDTH), 1.0, f32)
    for block in range(count):
        total = jnp.sum(partial[block * SUBLANES : (block + 1) * SUBLANES, :], axis=0, keepdims=True)
        least = jnp.minimum(least, total)
        finish(low + block, jnp.log2(total))

    @pl.when(jnp.min(least) < SMALLEST)
    def _():
        def exact(block, carry):
            def peaks(chunk, peak):
                return fold(jnp.maximum, peak, scores(low + block, chunk))

            peak = lax.fori_loop(0, chunks, peaks, jnp.full((ACC_ROWS, WIDTH), -jnp.inf, f32))
            top = jnp.max(peak, axis=0, keepdims=True)

            def sums(chunk, acc):
                return fold(jnp.add, acc, jnp.exp2(scores(low + block, chunk) - top))

            acc = lax.fori_loop(0, chunks, sums, zero)
            finish(low + block, top + jnp.log2(jnp.sum(acc, axis=0, keepdims=True)))
            return carry

        lax.fori_loop(0, count, exact, 0)


def pass_kernel(log_count, parts, prev, norm, main, tail, rhs, out, dual_out, full, edge, logs, partial):
    dual = combine(parts, log_count)
    dual_out[...] = dual
    bound = log_count - prev[...]
    fill_duals(dual, tail, full)
    fill_bounds(bound, edge, 0)
    column_logs(main, full, rhs, edge, logs, partial, 0, rhs.shape[1] // WIDTH)
    offset = bound if norm is None else bound - SCALE * norm[...]
    value = logs[...] + offset
    for i in range(out.shape[0]):
        out[i] = value


def place_of(index, shift, ring):
    return lax.rem(index[0] + (ring - shift), ring)


def source_block(value, at, xm, xt, xr, xn, edge):
    cells = value.shape[1]
    prepare_block(value, at, xm, xt, xr, xn, 2.0 * SCALE)
    rows = cells // LANES
    here = pl.ds(pl.multiple_of(at * rows, rows), rows)
    fill_bounds(SCALE * xn[here, :], edge, pl.multiple_of(at * cells, cells))


def first_kernel(x_ref, y_ref, ym, yt, yr, yn, yf, dual_out, xm, xt, xr, xn, logs, edge, partial):
    for at in range(y_ref.shape[0]):
        prepare_block(y_ref[at], at, ym, yt, yr, yn, 1.0)
    dual = -SCALE * yn[...]
    dual_out[...] = dual
    fill_duals(dual, yt, yf)
    source_block(x_ref[...], 0, xm, xt, xr, xn, edge)
    column_logs(ym, yf, xr, edge, logs, partial, 0, x_ref.shape[1] // WIDTH)


def second_kernel(ring, index, *refs):
    xs, refs = refs[: ring - 1], refs[ring - 1 :]
    ym, yf, own_m, own_t, own_r, own_n, own_logs = refs[:7]
    xm, xt, xr, xn, out, edge, logs, partial = refs[7:]
    cells, rows = own_m.shape[0], own_n.shape[0]
    at = place_of(index, 0, ring)
    here = pl.ds(pl.multiple_of(at * cells, cells), cells)
    xm[here, :] = own_m[...]
    xt[here, :] = own_t[...]
    xr[:, here] = own_r[...]
    here = pl.ds(pl.multiple_of(at * rows, rows), rows)
    xn[here, :] = own_n[...]
    logs[here, :] = own_logs[...]
    for shift, x_ref in enumerate(xs, 1):
        source_block(x_ref[...], place_of(index, shift, ring), xm, xt, xr, xn, edge)
    count = xs[0].shape[1] // WIDTH

    def block(shift, carry):
        column_logs(ym, yf, xr, edge, logs, partial, place_of(index, shift, ring) * count, count)
        return carry

    lax.fori_loop(1, ring, block, 0)
    value = logs[...] + SCALE * xn[...]
    for i in range(out.shape[0]):
        out[i] = value


def final_kernel(log_src, index, parts, dual, xn, col_out, row_out):
    blocks = col_out.shape[0]
    peers = parts.shape[0] // blocks
    for block in range(blocks):
        col_out[block] = combine(parts[block * peers : (block + 1) * peers], log_src) * (1.0 / SCALE)
    rows = row_out.shape[0]
    own = pl.ds(pl.multiple_of(index[0] * rows, rows), rows)
    row_out[...] = dual[own, :] * (1.0 / SCALE) + xn[own, :]


def params(mib):
    return pltpu.CompilerParams(vmem_limit_bytes=mib * 2**20)


def cost(rows, cols):
    pairs = rows * cols
    return pl.CostEstimate(flops=512 * pairs, bytes_accessed=pairs // 8, transcendentals=pairs)


def lse_pass(log_count, parts, prev, main, tail, rhs, copies, norm=None):
    length, width = main.shape[0], rhs.shape[1]
    norms = [] if norm is None else [norm]

    def kernel(parts, prev, *refs):
        at = len(norms)
        pass_kernel(log_count, parts, prev, refs[0] if at else None, *refs[at:])

    return pl.pallas_call(
        kernel,
        out_shape=(
            jax.ShapeDtypeStruct((copies, width // LANES, LANES), f32),
            jax.ShapeDtypeStruct((length // LANES, LANES), f32),
        ),
        in_specs=[vmem] * (5 + len(norms)),
        out_specs=(vmem, vmem),
        scratch_shapes=[
            pltpu.VMEM((length, LANES), bf16),
            pltpu.VMEM((EDGE, width), bf16),
            pltpu.VMEM((width // LANES, LANES), f32),
            pltpu.VMEM((width // WIDTH * SUBLANES, WIDTH), f32),
        ],
        compiler_params=params(9),
    )(parts, prev, *norms, main, tail, rhs)


def repeat_kernel(value, out):
    for i in range(out.shape[0]):
        out[i] = value[...]


def gathered(value, axes):
    copies = pl.pallas_call(
        repeat_kernel,
        out_shape=jax.ShapeDtypeStruct((lax.axis_size(axes),) + value.shape, value.dtype),
        in_specs=[vmem],
        out_specs=vmem,
        compiler_params=params(4),
    )(value)
    return lax.all_to_all(copies, axes, 0, 0, tiled=True)


def exchanged(parts, axes):
    return lax.all_to_all(parts, axes, 0, 0, tiled=True)


ROW_GATHER = "x"
COL_GATHER = ("z", "yl")
ROW_PEERS = ("yh", "core", "x")
COL_PEERS = ("z", "yl")
DEV = ("x", "z", "yl")


def on_device(x_feat, y_feat):
    ring = lax.axis_size(ROW_GATHER)
    index = lax.axis_index(ROW_GATHER).reshape(1)
    blocks = [x_feat]
    for shift in range(1, ring):
        pairs = [(i, (i + shift) % ring) for i in range(ring)]
        blocks.append(lax.ppermute(x_feat, ROW_GATHER, pairs))
    yg = gathered(y_feat, COL_GATHER)
    rows, cols = ring * x_feat.shape[1], yg.shape[0] * yg.shape[2]
    row_peers, col_peers = lax.axis_size(ROW_PEERS), lax.axis_size(COL_PEERS)
    log_tgt = math.log2(cols * row_peers)
    log_src = math.log2(rows * col_peers)

    def side(cells):
        return [
            jax.ShapeDtypeStruct((cells, LANES), bf16),
            jax.ShapeDtypeStruct((cells, LANES), bf16),
            jax.ShapeDtypeStruct((3 * x_feat.shape[0], cells), bf16),
            jax.ShapeDtypeStruct((cells // LANES, LANES), f32),
        ]

    def dual_of(cells):
        return jax.ShapeDtypeStruct((cells // LANES, LANES), f32)

    block = x_feat.shape[1]
    partial = pltpu.VMEM((block // WIDTH * SUBLANES, WIDTH), f32)
    ym, yt, yr, yn, yf, dual_y, *own = pl.pallas_call(
        first_kernel,
        out_shape=side(cols)
        + [jax.ShapeDtypeStruct((cols, LANES), bf16), dual_of(cols)]
        + side(block)
        + [dual_of(block)],
        in_specs=[vmem] * 2,
        out_specs=[vmem] * 11,
        scratch_shapes=[pltpu.VMEM((EDGE, block), bf16), partial],
        compiler_params=params(6),
        cost_estimate=cost(block, cols),
    )(x_feat, yg)
    xm, xt, xr, xn, sums = pl.pallas_call(
        lambda *refs: second_kernel(ring, *refs),
        out_shape=side(rows) + [jax.ShapeDtypeStruct((row_peers, rows // LANES, LANES), f32)],
        in_specs=[smem] + [vmem] * (ring + 6),
        out_specs=[vmem] * 5,
        scratch_shapes=[
            pltpu.VMEM((EDGE, rows), bf16),
            pltpu.VMEM((rows // LANES, LANES), f32),
            partial,
        ],
        compiler_params=params(6),
        cost_estimate=cost(rows - block, cols),
    )(index, *blocks[1:], ym, yf, *own)
    parts = exchanged(sums, ROW_PEERS)
    for iteration in range(1, ITERS):
        sums, dual_x = lse_pass(log_tgt, parts, dual_y, xm, xt, yr, col_peers)
        parts = exchanged(sums, COL_PEERS)
        sums, dual_y = lse_pass(log_src, parts, dual_x, ym, yt, xr, row_peers)
        parts = exchanged(sums, ROW_PEERS)
    sums, dual_x = lse_pass(log_tgt, parts, dual_y, xm, xt, yr, lax.axis_size(DEV), yn)
    parts = exchanged(sums, DEV)
    dual_col, dual_row = pl.pallas_call(
        lambda *refs: final_kernel(log_src, *refs),
        out_shape=(
            jax.ShapeDtypeStruct((ring, cols // LANES, LANES), f32),
            jax.ShapeDtypeStruct((x_feat.shape[1] // LANES, LANES), f32),
        ),
        in_specs=[smem] + [vmem] * 3,
        out_specs=(vmem, vmem),
        compiler_params=params(4),
    )(index, parts, dual_x, xn)
    return dual_row.reshape(-1), dual_col.reshape(-1)


def solution(mesh):
    fine = Mesh(mesh.devices.reshape(2, 2, 4, 4, 2), ("yh", "core", "x", "z", "yl"))
    in_specs = (P(None, DEV), P(None, ("yh", "core") + DEV))
    out_specs = (P(DEV), P(("yh", "core")))
    return jax.shard_map(
        on_device, mesh=fine, in_specs=in_specs, out_specs=out_specs, check_vma=False
    )
```

```python
import math

import jax
import jax.numpy as jnp
from jax import lax
from jax.experimental import pallas as pl
from jax.experimental.pallas import tpu as pltpu
from jax.sharding import Mesh
from jax.sharding import PartitionSpec as P

ITERS = 2
EPS = 0.5
LOG2E = 1.0 / math.log(2.0)
SCALE = LOG2E / EPS

LANES = 128
CHUNK = 256
WIDTH = 256
GROUP = 8
ACC_ROWS = 16
DUAL_LANE = 64
EDGE = 64
SUBLANES = 8
SMALLEST = 2.0**-80

f32 = jnp.float32
bf16 = jnp.bfloat16
vmem = pl.BlockSpec(memory_space=pltpu.VMEM)
smem = pl.BlockSpec(memory_space=pltpu.SMEM)


def split2(value):
    high = value.astype(bf16)
    return high, (value - high.astype(f32)).astype(bf16)


def fold(op, acc, value):
    rows = acc.shape[0]
    for i in range(value.shape[0] // rows):
        acc = op(acc, value[i * rows : (i + 1) * rows])
    return acc


def prepare_block(value, at, main, tail, rhs, norm, scale):
    dim, cells = value.shape
    rows = cells // LANES
    square = jnp.sum(value * value, axis=0, keepdims=True)
    for q in range(rows):
        norm[pl.ds(at * rows + q, 1), :] = square[:, q * LANES : (q + 1) * LANES]
    high, low = split2(value * scale)
    here = pl.ds(pl.multiple_of(at * cells, cells), cells)
    rhs[0:dim, here] = high
    rhs[dim : 2 * dim, here] = low
    rhs[2 * dim : 3 * dim, here] = high
    main[here, :] = jnp.transpose(jnp.concatenate([high, high], axis=0))
    tail[here, :] = jnp.transpose(jnp.concatenate([low, jnp.zeros_like(low)], axis=0))


def combine(parts, log_count):
    peak = parts[0]
    for i in range(1, parts.shape[0]):
        peak = jnp.maximum(peak, parts[i])
    total = jnp.exp2(parts[0] - peak)
    for i in range(1, parts.shape[0]):
        total = total + jnp.exp2(parts[i] - peak)
    return log_count - (peak + jnp.log2(total))


def split3(value):
    high = value.astype(bf16).astype(f32)
    mid = (value - high).astype(bf16).astype(f32)
    return high, mid, value - high - mid


def stacked(parts, row, ones):
    place = lax.broadcasted_iota(jnp.int32, (SUBLANES, LANES), 0)
    value = jnp.where(place < 6, 1.0, 0.0)
    for i, part in enumerate(parts):
        value = jnp.where(place == (3 - ones) + i, part[row : row + 1], value)
    return value


def fill_duals(dual, tail, full):
    parts = split3(dual)
    before = jnp.zeros((DUAL_LANE, LANES), f32)
    after = jnp.zeros((LANES - DUAL_LANE - SUBLANES, LANES), f32)
    for k in range(dual.shape[0]):
        here = pl.ds(k * LANES, LANES)
        rows = jnp.concatenate([before, stacked(parts, k, 3), after], axis=0)
        full[here, :] = (tail[here, :].astype(f32) + jnp.transpose(rows)).astype(bf16)


def fill_bounds(bound, edge, start):
    parts = split3(-bound)
    cells = bound.shape[0] * LANES
    edge[2 * SUBLANES :, pl.ds(start, cells)] = jnp.zeros((EDGE - 2 * SUBLANES, cells), bf16)
    for k in range(bound.shape[0]):
        rows = jnp.concatenate([stacked(parts, k, 0), jnp.zeros((SUBLANES, LANES), f32)], axis=0)
        edge[0 : 2 * SUBLANES, pl.ds(start + k * LANES, LANES)] = rows.astype(bf16)


def column_logs(main, full, rhs, edge, logs, partial, low, count):
    chunks = main.shape[0] // CHUNK
    rows_of = WIDTH // LANES

    def scores(block, chunk):
        here = pl.ds(chunk * CHUNK, CHUNK)
        if not isinstance(chunk, int):
            here = pl.ds(pl.multiple_of(chunk * CHUNK, CHUNK), CHUNK)
        cols = pl.ds(pl.multiple_of(block * WIDTH, WIDTH), WIDTH)
        lhs = jnp.concatenate([main[here, :], full[here, :]], axis=1)
        weight = jnp.concatenate([rhs[:, cols], edge[:, cols]], axis=0)
        return jnp.dot(lhs, weight, preferred_element_type=f32)

    def finish(block, value):
        for q in range(rows_of):
            logs[pl.ds(block * rows_of + q, 1), :] = value[:, q * LANES : (q + 1) * LANES]

    zero = jnp.zeros((ACC_ROWS, WIDTH), f32)

    size = min(GROUP, count)

    def step(group, carry):
        for t in range(size):
            block, acc = group * size + t, zero
            for chunk in range(chunks):
                acc = fold(jnp.add, acc, jnp.exp2(scores(low + block, chunk)))
            here = pl.ds(pl.multiple_of(block * SUBLANES, SUBLANES), SUBLANES)
            partial[here, :] = fold(jnp.add, acc[:SUBLANES], acc[SUBLANES:])
        return carry

    lax.fori_loop(0, count // size, step, 0)
    least = jnp.full((1, WIDTH), 1.0, f32)
    for block in range(count):
        total = jnp.sum(partial[block * SUBLANES : (block + 1) * SUBLANES, :], axis=0, keepdims=True)
        least = jnp.minimum(least, total)
        finish(low + block, jnp.log2(total))

    @pl.when(jnp.min(least) < SMALLEST)
    def _():
        def exact(block, carry):
            def peaks(chunk, peak):
                return fold(jnp.maximum, peak, scores(low + block, chunk))

            peak = lax.fori_loop(0, chunks, peaks, jnp.full((ACC_ROWS, WIDTH), -jnp.inf, f32))
            top = jnp.max(peak, axis=0, keepdims=True)

            def sums(chunk, acc):
                return fold(jnp.add, acc, jnp.exp2(scores(low + block, chunk) - top))

            acc = lax.fori_loop(0, chunks, sums, zero)
            finish(low + block, top + jnp.log2(jnp.sum(acc, axis=0, keepdims=True)))
            return carry

        lax.fori_loop(0, count, exact, 0)


def pass_kernel(log_count, parts, prev, norm, main, tail, rhs, out, dual_out, full, edge, logs, partial):
    dual = combine(parts, log_count)
    dual_out[...] = dual
    bound = log_count - prev[...]
    fill_duals(dual, tail, full)
    fill_bounds(bound, edge, 0)
    column_logs(main, full, rhs, edge, logs, partial, 0, rhs.shape[1] // WIDTH)
    offset = bound if norm is None else bound - SCALE * norm[...]
    value = logs[...] + offset
    for i in range(out.shape[0]):
        out[i] = value


def place_of(index, shift, ring):
    return lax.rem(index[0] + (ring - shift), ring)


def source_block(value, at, xm, xt, xr, xn, edge):
    cells = value.shape[1]
    prepare_block(value, at, xm, xt, xr, xn, 2.0 * SCALE)
    rows = cells // LANES
    here = pl.ds(pl.multiple_of(at * rows, rows), rows)
    fill_bounds(SCALE * xn[here, :], edge, pl.multiple_of(at * cells, cells))


def first_kernel(x_ref, y_ref, ym, yt, yr, yn, yf, dual_out, xm, xt, xr, xn, logs, edge, partial):
    for at in range(y_ref.shape[0]):
        prepare_block(y_ref[at], at, ym, yt, yr, yn, 1.0)
    dual = -SCALE * yn[...]
    dual_out[...] = dual
    fill_duals(dual, yt, yf)
    source_block(x_ref[...], 0, xm, xt, xr, xn, edge)
    column_logs(ym, yf, xr, edge, logs, partial, 0, x_ref.shape[1] // WIDTH)


def second_kernel(ring, index, *refs):
    xs, refs = refs[: ring - 1], refs[ring - 1 :]
    ym, yf, own_m, own_t, own_r, own_n, own_logs = refs[:7]
    xm, xt, xr, xn, out, edge, logs, partial = refs[7:]
    cells, rows = own_m.shape[0], own_n.shape[0]
    at = place_of(index, 0, ring)
    here = pl.ds(pl.multiple_of(at * cells, cells), cells)
    xm[here, :] = own_m[...]
    xt[here, :] = own_t[...]
    xr[:, here] = own_r[...]
    here = pl.ds(pl.multiple_of(at * rows, rows), rows)
    xn[here, :] = own_n[...]
    logs[here, :] = own_logs[...]
    for shift, x_ref in enumerate(xs, 1):
        source_block(x_ref[...], place_of(index, shift, ring), xm, xt, xr, xn, edge)
    count = xs[0].shape[1] // WIDTH

    def block(shift, carry):
        column_logs(ym, yf, xr, edge, logs, partial, place_of(index, shift, ring) * count, count)
        return carry

    lax.fori_loop(1, ring, block, 0)
    value = logs[...] + SCALE * xn[...]
    for i in range(out.shape[0]):
        out[i] = value


def final_kernel(log_src, index, parts, dual, xn, col_out, row_out):
    blocks = col_out.shape[0]
    peers = parts.shape[0] // blocks
    for block in range(blocks):
        col_out[block] = combine(parts[block * peers : (block + 1) * peers], log_src) * (1.0 / SCALE)
    rows = row_out.shape[0]
    own = pl.ds(pl.multiple_of(index[0] * rows, rows), rows)
    row_out[...] = dual[own, :] * (1.0 / SCALE) + xn[own, :]


def params(mib):
    return pltpu.CompilerParams(vmem_limit_bytes=mib * 2**20)


def cost(rows, cols):
    pairs = rows * cols
    return pl.CostEstimate(flops=512 * pairs, bytes_accessed=pairs // 8, transcendentals=pairs)


def lse_pass(log_count, parts, prev, main, tail, rhs, copies, norm=None):
    length, width = main.shape[0], rhs.shape[1]
    norms = [] if norm is None else [norm]

    def kernel(parts, prev, *refs):
        at = len(norms)
        pass_kernel(log_count, parts, prev, refs[0] if at else None, *refs[at:])

    return pl.pallas_call(
        kernel,
        out_shape=(
            jax.ShapeDtypeStruct((copies, width // LANES, LANES), f32),
            jax.ShapeDtypeStruct((length // LANES, LANES), f32),
        ),
        in_specs=[vmem] * (5 + len(norms)),
        out_specs=(vmem, vmem),
        scratch_shapes=[
            pltpu.VMEM((length, LANES), bf16),
            pltpu.VMEM((EDGE, width), bf16),
            pltpu.VMEM((width // LANES, LANES), f32),
            pltpu.VMEM((width // WIDTH * SUBLANES, WIDTH), f32),
        ],
        compiler_params=params(9),
    )(parts, prev, *norms, main, tail, rhs)


def repeat_kernel(value, out, done):
    copies = [pltpu.make_async_copy(value, out.at[i], done.at[i]) for i in range(out.shape[0])]
    for copy in copies:
        copy.start()
    for copy in copies:
        copy.wait()


def gathered(value, axes):
    count = lax.axis_size(axes)
    copies = pl.pallas_call(
        repeat_kernel,
        out_shape=jax.ShapeDtypeStruct((count,) + value.shape, value.dtype),
        in_specs=[pl.BlockSpec(memory_space=pl.ANY)],
        out_specs=pl.BlockSpec(memory_space=pl.ANY),
        scratch_shapes=[pltpu.SemaphoreType.DMA((count,))],
        compiler_params=params(4),
    )(value)
    return lax.all_to_all(copies, axes, 0, 0, tiled=True)


def exchanged(parts, axes):
    return lax.all_to_all(parts, axes, 0, 0, tiled=True)


ROW_GATHER = "x"
COL_GATHER = ("z", "yl")
ROW_PEERS = ("yh", "core", "x")
COL_PEERS = ("z", "yl")
DEV = ("x", "z", "yl")


def on_device(x_feat, y_feat):
    ring = lax.axis_size(ROW_GATHER)
    index = lax.axis_index(ROW_GATHER).reshape(1)
    blocks = [x_feat]
    for shift in range(1, ring):
        pairs = [(i, (i + shift) % ring) for i in range(ring)]
        blocks.append(lax.ppermute(x_feat, ROW_GATHER, pairs))
    yg = gathered(y_feat, COL_GATHER)
    rows, cols = ring * x_feat.shape[1], yg.shape[0] * yg.shape[2]
    row_peers, col_peers = lax.axis_size(ROW_PEERS), lax.axis_size(COL_PEERS)
    log_tgt = math.log2(cols * row_peers)
    log_src = math.log2(rows * col_peers)

    def side(cells):
        return [
            jax.ShapeDtypeStruct((cells, LANES), bf16),
            jax.ShapeDtypeStruct((cells, LANES), bf16),
            jax.ShapeDtypeStruct((3 * x_feat.shape[0], cells), bf16),
            jax.ShapeDtypeStruct((cells // LANES, LANES), f32),
        ]

    def dual_of(cells):
        return jax.ShapeDtypeStruct((cells // LANES, LANES), f32)

    block = x_feat.shape[1]
    partial = pltpu.VMEM((block // WIDTH * SUBLANES, WIDTH), f32)
    ym, yt, yr, yn, yf, dual_y, *own = pl.pallas_call(
        first_kernel,
        out_shape=side(cols)
        + [jax.ShapeDtypeStruct((cols, LANES), bf16), dual_of(cols)]
        + side(block)
        + [dual_of(block)],
        in_specs=[vmem] * 2,
        out_specs=[vmem] * 11,
        scratch_shapes=[pltpu.VMEM((EDGE, block), bf16), partial],
        compiler_params=params(6),
        cost_estimate=cost(block, cols),
    )(x_feat, yg)
    xm, xt, xr, xn, sums = pl.pallas_call(
        lambda *refs: second_kernel(ring, *refs),
        out_shape=side(rows) + [jax.ShapeDtypeStruct((row_peers, rows // LANES, LANES), f32)],
        in_specs=[smem] + [vmem] * (ring + 6),
        out_specs=[vmem] * 5,
        scratch_shapes=[
            pltpu.VMEM((EDGE, rows), bf16),
            pltpu.VMEM((rows // LANES, LANES), f32),
            partial,
        ],
        compiler_params=params(6),
        cost_estimate=cost(rows - block, cols),
    )(index, *blocks[1:], ym, yf, *own)
    parts = exchanged(sums, ROW_PEERS)
    for iteration in range(1, ITERS):
        sums, dual_x = lse_pass(log_tgt, parts, dual_y, xm, xt, yr, col_peers)
        parts = exchanged(sums, COL_PEERS)
        sums, dual_y = lse_pass(log_src, parts, dual_x, ym, yt, xr, row_peers)
        parts = exchanged(sums, ROW_PEERS)
    sums, dual_x = lse_pass(log_tgt, parts, dual_y, xm, xt, yr, lax.axis_size(DEV), yn)
    parts = exchanged(sums, DEV)
    dual_col, dual_row = pl.pallas_call(
        lambda *refs: final_kernel(log_src, *refs),
        out_shape=(
            jax.ShapeDtypeStruct((ring, cols // LANES, LANES), f32),
            jax.ShapeDtypeStruct((x_feat.shape[1] // LANES, LANES), f32),
        ),
        in_specs=[smem] + [vmem] * 3,
        out_specs=(vmem, vmem),
        compiler_params=params(4),
    )(index, parts, dual_x, xn)
    return dual_row.reshape(-1), dual_col.reshape(-1)


def solution(mesh):
    fine = Mesh(mesh.devices.reshape(2, 2, 4, 4, 2), ("yh", "core", "x", "z", "yl"))
    in_specs = (P(None, DEV), P(None, ("yh", "core") + DEV))
    out_specs = (P(DEV), P(("yh", "core")))
    return jax.shard_map(
        on_device, mesh=fine, in_specs=in_specs, out_specs=out_specs, check_vma=False
    )
```

```python
import math

import jax
import jax.numpy as jnp
from jax import lax
from jax.experimental import pallas as pl
from jax.experimental.pallas import tpu as pltpu
from jax.sharding import Mesh
from jax.sharding import PartitionSpec as P

ITERS = 2
EPS = 0.5
LOG2E = 1.0 / math.log(2.0)
SCALE = LOG2E / EPS

LANES = 128
CHUNK = 256
WIDTH = 256
GROUP = 8
ACC_ROWS = 16
DUAL_LANE = 64
EDGE = 64
SUBLANES = 8
SMALLEST = 2.0**-80

f32 = jnp.float32
bf16 = jnp.bfloat16
vmem = pl.BlockSpec(memory_space=pltpu.VMEM)
smem = pl.BlockSpec(memory_space=pltpu.SMEM)


def split2(value):
    high = value.astype(bf16)
    return high, (value - high.astype(f32)).astype(bf16)


def fold(op, acc, value):
    rows = acc.shape[0]
    for i in range(value.shape[0] // rows):
        acc = op(acc, value[i * rows : (i + 1) * rows])
    return acc


def prepare_block(value, at, main, tail, rhs, norm, scale):
    dim, cells = value.shape
    rows = cells // LANES
    square = jnp.sum(value * value, axis=0, keepdims=True)
    for q in range(rows):
        norm[pl.ds(at * rows + q, 1), :] = square[:, q * LANES : (q + 1) * LANES]
    high, low = split2(value * scale)
    here = pl.ds(pl.multiple_of(at * cells, cells), cells)
    rhs[0:dim, here] = high
    rhs[dim : 2 * dim, here] = low
    rhs[2 * dim : 3 * dim, here] = high
    main[here, :] = jnp.transpose(jnp.concatenate([high, high], axis=0))
    tail[here, :] = jnp.transpose(jnp.concatenate([low, jnp.zeros_like(low)], axis=0))


def combine(parts, log_count):
    peak = parts[0]
    for i in range(1, parts.shape[0]):
        peak = jnp.maximum(peak, parts[i])
    total = jnp.exp2(parts[0] - peak)
    for i in range(1, parts.shape[0]):
        total = total + jnp.exp2(parts[i] - peak)
    return log_count - (peak + jnp.log2(total))


def split3(value):
    high = value.astype(bf16).astype(f32)
    mid = (value - high).astype(bf16).astype(f32)
    return high, mid, value - high - mid


def stacked(parts, row, ones):
    place = lax.broadcasted_iota(jnp.int32, (SUBLANES, LANES), 0)
    value = jnp.where(place < 6, 1.0, 0.0)
    for i, part in enumerate(parts):
        value = jnp.where(place == (3 - ones) + i, part[row : row + 1], value)
    return value


def fill_duals(dual, tail, full):
    parts = split3(dual)
    before = jnp.zeros((DUAL_LANE, LANES), f32)
    after = jnp.zeros((LANES - DUAL_LANE - SUBLANES, LANES), f32)
    for k in range(dual.shape[0]):
        here = pl.ds(k * LANES, LANES)
        rows = jnp.concatenate([before, stacked(parts, k, 3), after], axis=0)
        full[here, :] = (tail[here, :].astype(f32) + jnp.transpose(rows)).astype(bf16)


def fill_bounds(bound, edge, start):
    parts = split3(-bound)
    cells = bound.shape[0] * LANES
    edge[2 * SUBLANES :, pl.ds(start, cells)] = jnp.zeros((EDGE - 2 * SUBLANES, cells), bf16)
    for k in range(bound.shape[0]):
        rows = jnp.concatenate([stacked(parts, k, 0), jnp.zeros((SUBLANES, LANES), f32)], axis=0)
        edge[0 : 2 * SUBLANES, pl.ds(start + k * LANES, LANES)] = rows.astype(bf16)


def column_logs(main, full, rhs, edge, logs, partial, place, count):
    chunks = main.shape[0] // CHUNK
    rows_of = WIDTH // LANES

    def scores(block, chunk):
        here = pl.ds(chunk * CHUNK, CHUNK)
        if not isinstance(chunk, int):
            here = pl.ds(pl.multiple_of(chunk * CHUNK, CHUNK), CHUNK)
        cols = pl.ds(pl.multiple_of(block * WIDTH, WIDTH), WIDTH)
        lhs = jnp.concatenate([main[here, :], full[here, :]], axis=1)
        weight = jnp.concatenate([rhs[:, cols], edge[:, cols]], axis=0)
        return jnp.dot(lhs, weight, preferred_element_type=f32)

    def finish(block, value):
        for q in range(rows_of):
            logs[pl.ds(block * rows_of + q, 1), :] = value[:, q * LANES : (q + 1) * LANES]

    zero = jnp.zeros((ACC_ROWS, WIDTH), f32)

    size = max(i for i in range(1, GROUP + 1) if count % i == 0)

    def step(group, carry):
        for t in range(size):
            block, acc = group * size + t, zero
            for chunk in range(chunks):
                acc = fold(jnp.add, acc, jnp.exp2(scores(place(block), chunk)))
            here = pl.ds(pl.multiple_of(block * SUBLANES, SUBLANES), SUBLANES)
            partial[here, :] = fold(jnp.add, acc[:SUBLANES], acc[SUBLANES:])
        return carry

    lax.fori_loop(0, count // size, step, 0)
    least = jnp.full((1, WIDTH), 1.0, f32)
    for block in range(count):
        total = jnp.sum(partial[block * SUBLANES : (block + 1) * SUBLANES, :], axis=0, keepdims=True)
        least = jnp.minimum(least, total)
        finish(place(block), jnp.log2(total))

    @pl.when(jnp.min(least) < SMALLEST)
    def _():
        def exact(block, carry):
            def peaks(chunk, peak):
                return fold(jnp.maximum, peak, scores(place(block), chunk))

            peak = lax.fori_loop(0, chunks, peaks, jnp.full((ACC_ROWS, WIDTH), -jnp.inf, f32))
            top = jnp.max(peak, axis=0, keepdims=True)

            def sums(chunk, acc):
                return fold(jnp.add, acc, jnp.exp2(scores(place(block), chunk) - top))

            acc = lax.fori_loop(0, chunks, sums, zero)
            finish(place(block), top + jnp.log2(jnp.sum(acc, axis=0, keepdims=True)))
            return carry

        lax.fori_loop(0, count, exact, 0)


def pass_kernel(log_count, parts, prev, norm, main, tail, rhs, out, dual_out, full, edge, logs, partial):
    dual = combine(parts, log_count)
    dual_out[...] = dual
    bound = log_count - prev[...]
    fill_duals(dual, tail, full)
    fill_bounds(bound, edge, 0)
    column_logs(main, full, rhs, edge, logs, partial, lambda i: i, rhs.shape[1] // WIDTH)
    offset = bound if norm is None else bound - SCALE * norm[...]
    value = logs[...] + offset
    for i in range(out.shape[0]):
        out[i] = value


def place_of(index, shift, ring):
    return lax.rem(index[0] + (ring - shift), ring)


def source_block(value, at, xm, xt, xr, xn, edge):
    cells = value.shape[1]
    prepare_block(value, at, xm, xt, xr, xn, 2.0 * SCALE)
    rows = cells // LANES
    here = pl.ds(pl.multiple_of(at * rows, rows), rows)
    fill_bounds(SCALE * xn[here, :], edge, pl.multiple_of(at * cells, cells))


def first_kernel(x_ref, y_ref, ym, yt, yr, yn, yf, dual_out, xm, xt, xr, xn, logs, edge, partial):
    for at in range(y_ref.shape[0]):
        prepare_block(y_ref[at], at, ym, yt, yr, yn, 1.0)
    dual = -SCALE * yn[...]
    dual_out[...] = dual
    fill_duals(dual, yt, yf)
    source_block(x_ref[...], 0, xm, xt, xr, xn, edge)
    column_logs(ym, yf, xr, edge, logs, partial, lambda i: i, x_ref.shape[1] // WIDTH)


def second_kernel(ring, index, *refs):
    xs, refs = refs[: ring - 1], refs[ring - 1 :]
    ym, yf, own_m, own_t, own_r, own_n, own_logs = refs[:7]
    xm, xt, xr, xn, out, edge, logs, partial = refs[7:]
    cells, rows = own_m.shape[0], own_n.shape[0]
    at = place_of(index, 0, ring)
    here = pl.ds(pl.multiple_of(at * cells, cells), cells)
    xm[here, :] = own_m[...]
    xt[here, :] = own_t[...]
    xr[:, here] = own_r[...]
    here = pl.ds(pl.multiple_of(at * rows, rows), rows)
    xn[here, :] = own_n[...]
    logs[here, :] = own_logs[...]
    for shift, x_ref in enumerate(xs, 1):
        source_block(x_ref[...], place_of(index, shift, ring), xm, xt, xr, xn, edge)
    count = xs[0].shape[1] // WIDTH

    def place(i):
        i = jnp.int32(i)
        return place_of(index, 1 + lax.div(i, jnp.int32(count)), ring) * count + lax.rem(i, jnp.int32(count))

    column_logs(ym, yf, xr, edge, logs, partial, place, (ring - 1) * count)
    value = logs[...] + SCALE * xn[...]
    for i in range(out.shape[0]):
        out[i] = value


def final_kernel(log_src, index, parts, dual, xn, col_out, row_out):
    blocks = col_out.shape[0]
    peers = parts.shape[0] // blocks
    for block in range(blocks):
        col_out[block] = combine(parts[block * peers : (block + 1) * peers], log_src) * (1.0 / SCALE)
    rows = row_out.shape[0]
    own = pl.ds(pl.multiple_of(index[0] * rows, rows), rows)
    row_out[...] = dual[own, :] * (1.0 / SCALE) + xn[own, :]


def params(mib):
    return pltpu.CompilerParams(vmem_limit_bytes=mib * 2**20)


def cost(rows, cols):
    pairs = rows * cols
    return pl.CostEstimate(flops=512 * pairs, bytes_accessed=pairs // 8, transcendentals=pairs)


def lse_pass(log_count, parts, prev, main, tail, rhs, copies, norm=None):
    length, width = main.shape[0], rhs.shape[1]
    norms = [] if norm is None else [norm]

    def kernel(parts, prev, *refs):
        at = len(norms)
        pass_kernel(log_count, parts, prev, refs[0] if at else None, *refs[at:])

    return pl.pallas_call(
        kernel,
        out_shape=(
            jax.ShapeDtypeStruct((copies, width // LANES, LANES), f32),
            jax.ShapeDtypeStruct((length // LANES, LANES), f32),
        ),
        in_specs=[vmem] * (5 + len(norms)),
        out_specs=(vmem, vmem),
        scratch_shapes=[
            pltpu.VMEM((length, LANES), bf16),
            pltpu.VMEM((EDGE, width), bf16),
            pltpu.VMEM((width // LANES, LANES), f32),
            pltpu.VMEM((width // WIDTH * SUBLANES, WIDTH), f32),
        ],
        compiler_params=params(9),
    )(parts, prev, *norms, main, tail, rhs)


def repeat_kernel(value, out, done):
    copies = [pltpu.make_async_copy(value, out.at[i], done.at[i]) for i in range(out.shape[0])]
    for copy in copies:
        copy.start()
    for copy in copies:
        copy.wait()


def gathered(value, axes):
    count = lax.axis_size(axes)
    copies = pl.pallas_call(
        repeat_kernel,
        out_shape=jax.ShapeDtypeStruct((count,) + value.shape, value.dtype),
        in_specs=[pl.BlockSpec(memory_space=pl.ANY)],
        out_specs=pl.BlockSpec(memory_space=pl.ANY),
        scratch_shapes=[pltpu.SemaphoreType.DMA((count,))],
        compiler_params=params(4),
    )(value)
    return lax.all_to_all(copies, axes, 0, 0, tiled=True)


def exchanged(parts, axes):
    return lax.all_to_all(parts, axes, 0, 0, tiled=True)


ROW_GATHER = "x"
COL_GATHER = ("z", "yl")
ROW_PEERS = ("yh", "core", "x")
COL_PEERS = ("z", "yl")
DEV = ("x", "z", "yl")


def on_device(x_feat, y_feat):
    ring = lax.axis_size(ROW_GATHER)
    index = lax.axis_index(ROW_GATHER).reshape(1)
    blocks = [x_feat]
    for shift in range(1, ring):
        pairs = [(i, (i + shift) % ring) for i in range(ring)]
        blocks.append(lax.ppermute(x_feat, ROW_GATHER, pairs))
    yg = gathered(y_feat, COL_GATHER)
    rows, cols = ring * x_feat.shape[1], yg.shape[0] * yg.shape[2]
    row_peers, col_peers = lax.axis_size(ROW_PEERS), lax.axis_size(COL_PEERS)
    log_tgt = math.log2(cols * row_peers)
    log_src = math.log2(rows * col_peers)

    def side(cells):
        return [
            jax.ShapeDtypeStruct((cells, LANES), bf16),
            jax.ShapeDtypeStruct((cells, LANES), bf16),
            jax.ShapeDtypeStruct((3 * x_feat.shape[0], cells), bf16),
            jax.ShapeDtypeStruct((cells // LANES, LANES), f32),
        ]

    def dual_of(cells):
        return jax.ShapeDtypeStruct((cells // LANES, LANES), f32)

    block = x_feat.shape[1]
    partial = pltpu.VMEM((block // WIDTH * SUBLANES, WIDTH), f32)
    ym, yt, yr, yn, yf, dual_y, *own = pl.pallas_call(
        first_kernel,
        out_shape=side(cols)
        + [jax.ShapeDtypeStruct((cols, LANES), bf16), dual_of(cols)]
        + side(block)
        + [dual_of(block)],
        in_specs=[vmem] * 2,
        out_specs=[vmem] * 11,
        scratch_shapes=[pltpu.VMEM((EDGE, block), bf16), partial],
        compiler_params=params(6),
        cost_estimate=cost(block, cols),
    )(x_feat, yg)
    xm, xt, xr, xn, sums = pl.pallas_call(
        lambda *refs: second_kernel(ring, *refs),
        out_shape=side(rows) + [jax.ShapeDtypeStruct((row_peers, rows // LANES, LANES), f32)],
        in_specs=[smem] + [vmem] * (ring + 6),
        out_specs=[vmem] * 5,
        scratch_shapes=[
            pltpu.VMEM((EDGE, rows), bf16),
            pltpu.VMEM((rows // LANES, LANES), f32),
            pltpu.VMEM(((rows - block) // WIDTH * SUBLANES, WIDTH), f32),
        ],
        compiler_params=params(6),
        cost_estimate=cost(rows - block, cols),
    )(index, *blocks[1:], ym, yf, *own)
    parts = exchanged(sums, ROW_PEERS)
    for iteration in range(1, ITERS):
        sums, dual_x = lse_pass(log_tgt, parts, dual_y, xm, xt, yr, col_peers)
        parts = exchanged(sums, COL_PEERS)
        sums, dual_y = lse_pass(log_src, parts, dual_x, ym, yt, xr, row_peers)
        parts = exchanged(sums, ROW_PEERS)
    sums, dual_x = lse_pass(log_tgt, parts, dual_y, xm, xt, yr, lax.axis_size(DEV), yn)
    parts = exchanged(sums, DEV)
    dual_col, dual_row = pl.pallas_call(
        lambda *refs: final_kernel(log_src, *refs),
        out_shape=(
            jax.ShapeDtypeStruct((ring, cols // LANES, LANES), f32),
            jax.ShapeDtypeStruct((x_feat.shape[1] // LANES, LANES), f32),
        ),
        in_specs=[smem] + [vmem] * 3,
        out_specs=(vmem, vmem),
        compiler_params=params(4),
    )(index, parts, dual_x, xn)
    return dual_row.reshape(-1), dual_col.reshape(-1)


def solution(mesh):
    fine = Mesh(mesh.devices.reshape(2, 2, 4, 4, 2), ("yh", "core", "x", "z", "yl"))
    in_specs = (P(None, DEV), P(None, ("yh", "core") + DEV))
    out_specs = (P(DEV), P(("yh", "core")))
    return jax.shard_map(
        on_device, mesh=fine, in_specs=in_specs, out_specs=out_specs, check_vma=False
    )
```
